512 devices in a mesh: ctx: 16 (over y, z_lo), tp: 32 (over x, z_hi, core).
Axes of the slice: x: 4, y: 8, z: 8 (z_hi: 4, z_lo: 2; z = z_hi * 2 + z_lo), core: 2. Of those that a mesh axis runs over, the one named last changes fastest.
Arguments:
- x_in: bfloat16 [8192, 16384], P('ctx', 'tp'), may hold values from -6 to 6
- bc_in: bfloat16 [8192, 4096], P(('ctx', 'tp')), may hold values from -6 to 6
- conv_x: float32 [4, 16384], P(None, 'tp'), may hold values from -3 to 3
- conv_bc: float32 [4, 4096], replicated, may hold values from -3 to 3
- log_decay: float32 [8192, 256], P('ctx', 'tp'), may hold values from -2 to 0, as said below
- grad_y: bfloat16 [8192, 16384], P('ctx', 'tp'), may hold values from -0.009765625 to 0.009765625
Outputs:
- grad_x: bfloat16 [8192, 16384], P('ctx', 'tp')
- grad_bc: float32 [8192, 4096], P(('ctx', 'tp'))
- grad_decay: float32 [8192, 256], P('ctx', 'tp')
The draws below stay inside these ranges and needn't reach their ends.
Inputs may be any that keep to these rules, and one draw needn't show every extreme that they name: `log_decay`: each entry is the logarithm of a decay factor of one head at one token.
All inputs are finite; a program needn't handle non-finite values.
Results may differ from the reference program's by a relative error of at most 0.00205.
Values may be sent and summed in bfloat16 or wider, within the bound.
No kernel may reach another device: no remote copies, remote signals or barrier semaphores. Data moves between devices by JAX's collectives and lax.ppermute only.
A program may use at most 128 MiB of HBM per device.

```python
import math
import jax
import jax.numpy as jnp
from jax import lax

HEAD_DIM = 64
STATE = 256
CONV = 4
HEADS_GROUP = 32
HEAD_DEV = 8
BLOCK = 256
TOTAL_HEADS = 256
GROUPS = 8
SEQUENCE_TOKENS = 8192


def draw_log_decay(key, part):
    key = jax.random.fold_in(key, 7)
    key_kind, key_fast, key_slow, key_rough, main_spike_position, main_spike_height = jax.random.split(key, 6)
    fast_share = 5
    fast_heads = jax.random.randint(key_kind, (TOTAL_HEADS,), 0, 10) < fast_share
    fast_rates = jnp.exp(jax.random.uniform(key_fast, (TOTAL_HEADS,), jnp.float32, math.log(0.05), math.log(0.1)))
    slow_rates = jnp.exp(jax.random.uniform(key_slow, (TOTAL_HEADS,), jnp.float32, math.log(0.05), math.log(0.5))) / SEQUENCE_TOKENS
    decay_speeds = jnp.where(fast_heads, fast_rates, slow_rates)
    jitter_level = jnp.exp(jax.random.uniform(key_rough, (SEQUENCE_TOKENS, TOTAL_HEADS), jnp.float32, -math.log(2.0), math.log(2.0)))
    spike_positions = jax.random.randint(main_spike_position, (2,), 0, SEQUENCE_TOKENS)
    spike_heights = jnp.log(1.0 - jax.random.uniform(main_spike_height, (2, TOTAL_HEADS), jnp.float32, 0.2, 0.5))
    token_positions = jnp.arange(SEQUENCE_TOKENS, dtype=jnp.int32)[:, None]
    spike_log_values = jnp.where(token_positions == spike_positions[0], spike_heights[0][None, :], 0.0)
    spike_log_values = spike_log_values + jnp.where(token_positions == spike_positions[1], spike_heights[1][None, :], 0.0)
    return -decay_speeds[None, :] * jitter_level + spike_log_values


def shard_levels(own_key, dims, cuts, smallest, largest):
    level = 1.0
    for dim, blocks in cuts:
        heights = jax.random.uniform(jax.random.fold_in(jax.random.fold_in(own_key, 6), dim), (blocks,), jnp.float32, smallest / len(cuts), largest / len(cuts))
        level = level * jnp.repeat(jnp.exp(heights), dims[dim] // blocks).reshape((-1,) + (1,) * (len(dims) - 1 - dim))
    return level


def bell_draw(key, dims, spread, most, cuts=(), kind=jnp.bfloat16):
    result = spread * jax.random.normal(key, dims, jnp.float32)
    if cuts:
        result = result * shard_levels(key, dims, cuts, -0.22, 0.18)
    return jnp.clip(result, -most, most).astype(kind)


def setup_inputs(seed: int = 0) -> dict:
    arg_keys = jax.random.split(jax.random.key(seed), 7)
    return {
        "x_in": bell_draw(arg_keys[0], (SEQUENCE_TOKENS, TOTAL_HEADS * HEAD_DIM), 1.0, 6.0, ((0, 16), (1, 32))),
        "bc_in": bell_draw(arg_keys[1], (SEQUENCE_TOKENS, 2 * GROUPS * STATE), 1.0, 6.0, ((0, 512),)),
        "conv_x": bell_draw(arg_keys[2], (CONV, TOTAL_HEADS * HEAD_DIM), CONV ** -0.5, 3.0, ((1, 32),), jnp.float32),
        "conv_bc": bell_draw(arg_keys[3], (CONV, 2 * GROUPS * STATE), CONV ** -0.5, 3.0, (), jnp.float32),
        "log_decay": draw_log_decay(jax.random.fold_in(arg_keys[6], 71), 0),
        "grad_y": bell_draw(arg_keys[5], (SEQUENCE_TOKENS, TOTAL_HEADS * HEAD_DIM), (0.0625 / SEQUENCE_TOKENS ** 0.5), 0.009765625, ((0, 16), (1, 32))),
    }


def causal_conv(values, conv_taps):
    row_count = values.shape[0]
    padded = jnp.pad(values, ((CONV - 1, 0), (0, 0)))
    summed = conv_taps[0] * padded[0:row_count]
    for offset in range(1, CONV):
        summed = summed + conv_taps[offset] * padded[offset:offset + row_count]
    return summed

def block_pass(carried_state, pieces):
    inputs, key_acts, queries, log_rates = pieces
    span_rows = log_rates.shape[0]
    cumulative = jnp.cumsum(log_rates, axis=0)
    row_index = jnp.arange(span_rows, dtype=jnp.int32)[:, None]
    col_index = jnp.arange(span_rows, dtype=jnp.int32)[None, :]
    causal = (row_index >= col_index)[:, :, None]
    gap_logs = jnp.where(causal, cumulative[:, None, :] - cumulative[None, :, :], 0.0)
    mixing = jnp.where(causal, jnp.exp(gap_logs), 0.0)
    scores = jnp.dot(queries, key_acts.T, preferred_element_type=jnp.float32, precision=lax.Precision.HIGHEST)
    within = jnp.einsum('ijh,jhp->ihp', mixing * scores[:, :, None], inputs, precision=lax.Precision.HIGHEST)
    carried = jnp.einsum('in,hpn->ihp', queries, carried_state, precision=lax.Precision.HIGHEST) * jnp.exp(cumulative)[:, :, None]
    last_log = cumulative[-1]
    fading = jnp.exp(last_log[None, :] - cumulative)
    added = jnp.einsum('jhp,jn->hpn', inputs * fading[:, :, None], key_acts, precision=lax.Precision.HIGHEST)
    new_state = jnp.exp(last_log)[:, None, None] * carried_state + added
    return (new_state, within + carried)

def state_space(inputs, key_acts, queries, log_rates, carried_state):
    row_count = inputs.shape[0]
    head_count = log_rates.shape[1]
    block_count = row_count // BLOCK
    shaped = (inputs.reshape(block_count, BLOCK, head_count, HEAD_DIM), key_acts.reshape(block_count, BLOCK, STATE), queries.reshape(block_count, BLOCK, STATE), log_rates.reshape(block_count, BLOCK, head_count))
    final_state, outputs = lax.scan(block_pass, carried_state, shaped)
    return (outputs.reshape(row_count, head_count * HEAD_DIM), final_state)

def reference(x_in, bc_in, conv_x, conv_bc, log_decay, grad_y):
    tokens = x_in.shape[0]
    col_width = HEAD_DEV * HEAD_DIM

    def bc_forward(raw_cols):
        return jax.nn.silu(causal_conv(raw_cols, conv_bc))
    bc_act, bc_pullback = jax.vjp(bc_forward, bc_in.astype(jnp.float32))

    def one_group(summed, group_index):
        col_start = (group_index * col_width).astype(jnp.int32)
        head_start = (group_index * HEAD_DEV).astype(jnp.int32)
        bc_start = (group_index * HEAD_DEV // HEADS_GROUP * (2 * STATE)).astype(jnp.int32)
        pair = lax.dynamic_slice_in_dim(bc_act, bc_start, 2 * STATE, 1)
        key_acts = pair[:, :STATE]
        queries = pair[:, STATE:]
        raw_cols = lax.dynamic_slice_in_dim(x_in, col_start, col_width, 1).astype(jnp.float32)
        conv_taps = lax.dynamic_slice_in_dim(conv_x, col_start, col_width, 1)
        log_rates = lax.dynamic_slice_in_dim(log_decay, head_start, HEAD_DEV, 1)
        cotangent = lax.dynamic_slice_in_dim(grad_y, col_start, col_width, 1).astype(jnp.float32)

        def forward(values, keys_in, queries_in, logs_in):
            act_block = jax.nn.silu(causal_conv(values, conv_taps))
            start_state = jnp.zeros((HEAD_DEV, HEAD_DIM, STATE), jnp.float32)
            outputs, final_state = state_space(act_block, keys_in, queries_in, logs_in, start_state)
            return outputs
        outputs, pullback = jax.vjp(forward, raw_cols, key_acts, queries, log_rates)
        grad_raw, grad_keys, grad_queries, grad_logs = pullback(cotangent)
        current = lax.dynamic_slice_in_dim(summed, bc_start, 2 * STATE, 1)
        summed = lax.dynamic_update_slice_in_dim(summed, current + jnp.concatenate([grad_keys, grad_queries], axis=1), bc_start, 1)
        return (summed, (grad_raw.astype(jnp.bfloat16), grad_logs))
    group_count = TOTAL_HEADS // HEAD_DEV
    summed, (grad_blocks, decay_blocks) = lax.scan(one_group, jnp.zeros((tokens, 2 * GROUPS * STATE), jnp.float32), jnp.arange(group_count, dtype=jnp.int32))
    grad_x = jnp.transpose(grad_blocks, (1, 0, 2)).reshape(tokens, TOTAL_HEADS * HEAD_DIM)
    grad_decay = jnp.transpose(decay_blocks, (1, 0, 2)).reshape(tokens, TOTAL_HEADS)
    grad_bc = bc_pullback(summed)[0]
    return (grad_x, grad_bc, grad_decay)
```

```python
import functools

import jax
import jax.numpy as jnp
from jax import lax
from jax.experimental import pallas as pl
from jax.experimental.pallas import tpu as pltpu
from jax.sharding import Mesh, PartitionSpec as P

HEAD_DIM = 64
STATE = 256
CONV = 4
HEADS = 8
BLOCK = 256
ROWS = 512
COLS = HEADS * HEAD_DIM
BLOCKS = ROWS // BLOCK
HALO = 16
META = 128

F32 = jnp.float32
BF16 = jnp.bfloat16
NN = ((1,), (0,))
NT = ((1,), (1,))
TN = ((0,), (0,))
CTX = ("y", "zl")
TP = ("x", "zh", "core")


def mul(a, b, dims):
    return lax.dot_general(a, b, (dims, ((), ())), preferred_element_type=F32)


def split2(a):
    high = a.astype(BF16)
    return high, (a - high.astype(F32)).astype(BF16)


def split3(a):
    high = a.astype(BF16)
    rest = a - high.astype(F32)
    middle = rest.astype(BF16)
    return high, middle, (rest - middle.astype(F32)).astype(BF16)


def dot3(a, b, dims):
    return mul(a[0], b[0], dims) + (mul(a[0], b[1], dims) + mul(a[1], b[0], dims))


def exact_left(ones, b, dims):
    parts = split3(b)
    return mul(ones, parts[0], dims) + (mul(ones, parts[1], dims) + mul(ones, parts[2], dims))


def exact_right(a, ones, dims):
    parts = split3(a)
    return mul(parts[0], ones, dims) + (mul(parts[1], ones, dims) + mul(parts[2], ones, dims))


def expander(rows):
    head = lax.broadcasted_iota(jnp.int32, (rows, COLS), 0)
    col = lax.broadcasted_iota(jnp.int32, (rows, COLS), 1)
    return jnp.where((col >= head * HEAD_DIM) & (col < (head + 1) * HEAD_DIM), 1.0, 0.0).astype(BF16)


def row_col(shape=(BLOCK, BLOCK)):
    return (
        lax.broadcasted_iota(jnp.int32, shape, 0),
        lax.broadcasted_iota(jnp.int32, shape, 1),
    )


def sigmoid(v):
    return 1.0 / (1.0 + jnp.exp(-v))


def conv_silu(buf, prev, rows, taps):
    buf[0:8] = prev[HALO - 8 :].astype(F32)
    buf[8 : 8 + ROWS] = rows[...].astype(F32)
    pre = taps[0:1] * buf[5 : 5 + ROWS]
    for k in range(1, CONV):
        pre = pre + taps[k : k + 1] * buf[5 + k : 5 + k + ROWS]
    gate = sigmoid(pre)
    return pre * gate, gate * (1.0 + pre * (1.0 - gate))


def feature_kernel(x_ref, prev_ref, taps_ref, log_ref, grad_ref,
                   act_ref, slope_ref, fade_ref, grown_ref, cum_ref, cumt_ref, buf):
    act, slope = conv_silu(buf, prev_ref, x_ref, taps_ref)
    act_ref[...] = act
    slope_ref[...] = slope
    row, col = row_col()
    upper = jnp.where(row <= col, 1.0, 0.0).astype(BF16)
    lower = jnp.where(col <= row, 1.0, 0.0).astype(BF16)
    spread = expander(META)
    for b in range(BLOCKS):
        part = slice(b * BLOCK, (b + 1) * BLOCK)
        logs = log_ref[part]
        cum = exact_left(lower, logs, NN)
        cum_ref[part] = cum
        cumt_ref[b] = exact_right(logs, upper, TN)[0:8]
        last = cum[BLOCK - 1 : BLOCK]
        fade_ref[part] = exact_right(jnp.exp(last - cum), spread, NN)
        grown_ref[part] = grad_ref[part].astype(F32) * exact_right(jnp.exp(cum), spread, NN)


def power_scale(rows):
    top = jnp.max(jnp.abs(rows), axis=1, keepdims=True)
    return jnp.clip(14.0 - jnp.ceil(jnp.log2(jnp.maximum(top, 1e-30))), -100.0, 100.0)


def pack_rows(first, second, out, logs=None):
    lane = lax.broadcasted_iota(jnp.int32, (first.shape[0], META), 1)
    up_first = power_scale(first)
    up_second = power_scale(second)
    out[:, 0:COLS] = first * jnp.exp2(up_first)
    out[:, COLS : 2 * COLS] = second * jnp.exp2(up_second)
    meta = jnp.where(lane == 16, up_first, jnp.where(lane == 17, up_second, 0.0))
    if logs is not None:
        meta = jnp.where(lane < 16, logs, meta)
    out[:, 2 * COLS :] = meta


def state_kernel(bc_ref, prev_ref, taps_ref, act_ref, fade_ref, grown_ref, cum_ref,
                 bc_act_ref, slope_ref, early_ref, late_ref, pack_ref, buf):
    act, slope = conv_silu(buf, prev_ref, bc_ref, taps_ref)
    bc_act_ref[...] = act
    slope_ref[...] = slope
    spread = expander(META)
    states, grads, decays = [], [], []
    total = jnp.zeros((1, META), F32)
    for b in range(BLOCKS):
        part = slice(b * BLOCK, (b + 1) * BLOCK)
        keys = split2(act[part, 0:STATE])
        queries = split2(act[part, STATE:])
        states.append(dot3(keys, split2(act_ref[part] * fade_ref[part]), TN))
        grads.append(dot3(queries, split2(grown_ref[part]), TN))
        last = cum_ref[(b + 1) * BLOCK - 1 : (b + 1) * BLOCK]
        total = total + last
        decays.append(exact_right(jnp.broadcast_to(jnp.exp(last), (8, META)), spread, NN)[0:1])
    early_ref[...] = states[0]
    late_ref[...] = grads[1]
    state = decays[1] * states[0] + states[1]
    grad = grads[0] + decays[0] * grads[1]
    high = total.astype(BF16).astype(F32)
    low = total - high
    lane = lax.broadcasted_iota(jnp.int32, (1, META), 1)
    logs = jnp.where(lane < 8, high, pltpu.roll(low, 8, 1))
    pack_rows(state, grad, pack_ref, jnp.where(lane < 16, logs, 0.0))


def scan_kernel(places, got_ref, out_ref):
    piece = STATE // places
    spread = expander(META)
    lane = lax.broadcasted_iota(jnp.int32, (8, META), 1)

    def rows(p):
        return slice(p * piece, (p + 1) * piece)

    decays = []
    for p in range(places):
        meta = got_ref[p * piece : p * piece + 8, 2 * COLS :]
        logs = meta + pltpu.roll(meta, META - 8, 1)
        decay = jnp.where(lane < 8, jnp.exp(jnp.minimum(logs, 0.0)), 0.0)
        decays.append(exact_right(decay, spread, NN)[0:1])

    def part(p, which):
        up = got_ref[rows(p), 2 * COLS + 16 + which : 2 * COLS + 17 + which]
        return got_ref[rows(p), which * COLS : (which + 1) * COLS] * jnp.exp2(-up)

    coming = jnp.zeros((piece, COLS), F32)
    befores = []
    for p in range(places):
        befores.append(coming)
        coming = decays[p] * coming + part(p, 0)
    going = jnp.zeros((piece, COLS), F32)
    for p in reversed(range(places)):
        pack_rows(befores[p], going, out_ref.at[rows(p)])
        going = decays[p] * going + part(p, 1)


def block_kernel(act_ref, grad_ref, bc_ref, cum_ref, cumt_ref, dx_ref, dbc_ref, dlog_ref):
    row, col = row_col()
    causal = row <= col
    later = jnp.where(col >= row, 1.0, 0.0).astype(BF16)
    keys = split2(bc_ref[:, 0:STATE])
    queries = split2(bc_ref[:, STATE:])
    scores = dot3(keys, queries, NT)
    total = jnp.zeros((BLOCK, BLOCK), F32)
    across, down = [], []
    for h in range(HEADS):
        cols = slice(h * HEAD_DIM, (h + 1) * HEAD_DIM)
        gap = cumt_ref[0, h : h + 1, :] - cum_ref[:, h : h + 1]
        mixing = jnp.where(causal, jnp.exp(jnp.where(causal, gap, 0.0)), 0.0)
        grads = grad_ref[:, cols]
        values = split2(act_ref[:, cols])
        pairs = mixing * (mul(values[0], grads, NT) + mul(values[1], grads, NT))
        total = total + pairs
        weights = pairs * scores
        across.append(jnp.sum(weights, axis=0, keepdims=True))
        down.append(jnp.sum(weights, axis=1, keepdims=True))
        mixed = split2(mixing * scores)
        dx_ref[:, cols] = mul(mixed[0], grads, NN) + mul(mixed[1], grads, NN)
    pairs = split2(total)
    dbc_ref[:, 0:STATE] = dot3(pairs, queries, NN)
    dbc_ref[:, STATE:] = dot3(pairs, keys, TN)
    dlog_ref[...] = exact_left(later, jnp.concatenate(across, axis=0), NT) - exact_left(
        later, jnp.concatenate(down, axis=1), NN
    )


def carry_kernel(got_ref, early_ref, late_ref, act_ref, xslope_ref, fade_ref, grown_ref, cum_ref,
                 bc_ref, bslope_ref, dx_ref, dbc_ref, dlog_ref,
                 gx_ref, gbc_ref, glog_ref):
    row, col = row_col()
    later = jnp.where(col >= row, 1.0, 0.0).astype(BF16)
    before = jnp.where(col < row, 1.0, 0.0).astype(BF16)
    spread = expander(META)
    coming = got_ref[:, 0:COLS] * jnp.exp2(-got_ref[:, 2 * COLS + 16 : 2 * COLS + 17])
    going = got_ref[:, COLS : 2 * COLS] * jnp.exp2(-got_ref[:, 2 * COLS + 17 : 2 * COLS + 18])
    decays = []
    for b in range(BLOCKS):
        last = cum_ref[(b + 1) * BLOCK - 1 : (b + 1) * BLOCK]
        decays.append(exact_right(jnp.broadcast_to(jnp.exp(last), (8, META)), spread, NN)[0:1])
    comings = [coming, decays[0] * coming + early_ref[...]]
    goings = [decays[1] * going + late_ref[...], going]
    for b in range(BLOCKS):
        part = slice(b * BLOCK, (b + 1) * BLOCK)
        enter = split2(comings[b])
        leave = split2(goings[b])
        keys = split2(bc_ref[part, 0:STATE])
        queries = split2(bc_ref[part, STATE:])
        fade = fade_ref[part]
        grown = grown_ref[part]
        faded = act_ref[part] * fade
        reads = dot3(queries, enter, NN)
        pulls = dot3(keys, leave, NN)
        gx_ref[part] = (dx_ref[part] + fade * pulls) * xslope_ref[part]
        faded2 = split2(faded)
        grown2 = split2(grown)
        gbc_ref[part, 0:STATE] = (dbc_ref[part, 0:STATE] + dot3(faded2, leave, NT)) * bslope_ref[part, 0:STATE]
        gbc_ref[part, STATE:] = (dbc_ref[part, STATE:] + dot3(grown2, enter, NT)) * bslope_ref[part, STATE:]
        across = exact_right(grown * reads, spread, NT)
        down = exact_right(faded * pulls, spread, NT)
        both = jnp.sum(comings[b] * goings[b], axis=0, keepdims=True) * decays[b]
        both = exact_right(jnp.broadcast_to(both, (8, COLS)), spread, NT)[0:1]
        found = exact_left(later, across, NN) + exact_left(before, down, NN) + both
        glog_ref[part] = dlog_ref[part] + found[:, 0:HEADS]


def back_conv(buf, rows, halo, taps):
    buf[0:ROWS] = rows[...]
    buf[ROWS : ROWS + 8] = halo[...]
    out = taps[0:1] * buf[3 : 3 + ROWS]
    for k in range(1, CONV):
        out = out + taps[k : k + 1] * buf[3 - k : 3 - k + ROWS]
    return out


def grad_bc_kernel(rows_ref, halo_ref, taps_ref, out_ref, buf):
    out_ref[...] = back_conv(buf, rows_ref, halo_ref, taps_ref)


def grad_x_kernel(rows_ref, halo_ref, taps_ref, out_ref, buf):
    out_ref[...] = back_conv(buf, rows_ref, halo_ref, taps_ref).astype(BF16)


def call(kernel, outs, scratch=(), flops=1 << 26, size=1 << 22, **more):
    return pl.pallas_call(
        kernel,
        out_shape=[jax.ShapeDtypeStruct(shape, dtype) for shape, dtype in outs],
        scratch_shapes=list(scratch),
        compiler_params=pltpu.CompilerParams(vmem_limit_bytes=48 * 2**20),
        cost_estimate=pl.CostEstimate(flops=flops, bytes_accessed=size, transcendentals=0),
        **more,
    )


def shifted(array, by):
    devices = lax.axis_size(CTX)
    pairs = [(i, i + by) for i in range(devices) if 0 <= i + by < devices]
    return lax.ppermute(array, CTX, pairs)


def per_device(x_in, bc_in, conv_x, conv_bc, log_decay, grad_y):
    core = lax.axis_index("core")
    owners = lax.axis_size(("x", "zh"))
    places = lax.axis_size(CTX)
    groups = bc_in.shape[1] // (2 * STATE)
    own = bc_in.shape[0]
    fan = owners // groups
    group = lax.axis_index(("x", "zh")) // fan
    taps_bc = lax.dynamic_slice_in_dim(conv_bc, group * (2 * STATE), 2 * STATE, 1)
    swap = [(0, 1), (1, 0)]

    spread = jnp.broadcast_to(
        bc_in.reshape(own, groups, 1, 2 * STATE).transpose(1, 2, 0, 3), (groups, fan, own, 2 * STATE)
    ).reshape(owners, own, 2 * STATE)
    mine = lax.all_to_all(spread, ("x", "zh"), 0, 0, tiled=True)
    theirs = lax.ppermute(mine, "core", swap)
    bc_rows = jnp.where(
        core == 0, jnp.stack([mine, theirs], 1), jnp.stack([theirs, mine], 1)
    ).reshape(ROWS, 2 * STATE)

    x_prev = shifted(x_in[ROWS - HALO :], 1)
    bc_prev = shifted(bc_rows[ROWS - HALO :], 1)
    logs = jnp.pad(log_decay, ((0, 0), (0, META - HEADS)))
    wide = (ROWS, COLS)
    act, xslope, fade, grown, cum, cumt = call(
        feature_kernel,
        [(wide, F32)] * 4 + [((ROWS, META), F32), ((BLOCKS, 8, BLOCK), F32)],
        [pltpu.VMEM((ROWS + 8, COLS), F32)],
    )(x_in, x_prev, conv_x, logs, grad_y)
    packed = (STATE, 2 * COLS + META)
    bc_act, bslope, early, late, sent = call(
        state_kernel,
        [((ROWS, 2 * STATE), F32)] * 2 + [((STATE, COLS), F32)] * 2 + [(packed, F32)],
        [pltpu.VMEM((ROWS + 8, COLS), F32)],
    )(bc_rows, bc_prev, taps_bc, act, fade, grown, cum)
    got = lax.all_to_all(sent.astype(jnp.float16), CTX, 0, 0, tiled=True)

    def rows_of(width):
        return pl.BlockSpec((BLOCK, width), lambda b: (b, 0))

    dx, dbc, dlog = call(
        block_kernel,
        [(wide, F32), ((ROWS, 2 * STATE), F32), ((ROWS, HEADS), F32)],
        grid=(BLOCKS,),
        in_specs=[
            rows_of(COLS), rows_of(COLS), rows_of(2 * STATE), rows_of(META),
            pl.BlockSpec((1, 8, BLOCK), lambda b: (b, 0, 0)),
        ],
        out_specs=[rows_of(COLS), rows_of(2 * STATE), rows_of(HEADS)],
    )(act, grad_y, bc_act, cum, cumt)

    (back,) = call(functools.partial(scan_kernel, places), [(packed, F32)])(got.astype(F32))
    carried = lax.all_to_all(back.astype(jnp.float16), CTX, 0, 0, tiled=True).astype(F32)

    gx, gbc, glog = call(
        carry_kernel, [(wide, F32), ((ROWS, 2 * STATE), F32), ((ROWS, HEADS), F32)]
    )(carried, early, late, act, xslope, fade, grown, cum, bc_act, bslope, dx, dbc, dlog)

    bc_later = shifted(gbc[:8], -1)
    x_later = shifted(gx[:8], -1)
    (terms,) = call(
        grad_bc_kernel, [((ROWS, 2 * STATE), F32)], [pltpu.VMEM((ROWS + 8, 2 * STATE), F32)]
    )(gbc, bc_later, taps_bc)
    terms = terms.reshape(owners, 2, own, 2 * STATE)
    keep = lax.dynamic_index_in_dim(terms, core, 1, False)
    give = lax.dynamic_index_in_dim(terms, 1 - core, 1, False)
    summed = keep + lax.ppermute(give, "core", swap)
    parts = lax.all_to_all(summed, ("x", "zh"), 0, 0, tiled=True)
    grad_bc = jnp.sum(parts.reshape(groups, fan, own, 2 * STATE), axis=1)
    grad_bc = grad_bc.transpose(1, 0, 2).reshape(own, groups * 2 * STATE)
    (grad_x,) = call(
        grad_x_kernel, [(wide, BF16)], [pltpu.VMEM((ROWS + 8, COLS), F32)]
    )(gx, x_later, conv_x)
    return grad_x, grad_bc, glog


def solution(mesh):
    fine = Mesh(mesh.devices.reshape(8, 2, 4, 4, 2), CTX + TP)
    return jax.shard_map(
        per_device,
        mesh=fine,
        in_specs=(P(CTX, TP), P(CTX + TP, None), P(None, TP), P(), P(CTX, TP), P(CTX, TP)),
        out_specs=(P(CTX, TP), P(CTX + TP, None), P(CTX, TP)),
        check_vma=False,
    )
```

```python
import functools

import jax
import jax.numpy as jnp
from jax import lax
from jax.experimental import pallas as pl
from jax.experimental.pallas import tpu as pltpu
from jax.sharding import Mesh, PartitionSpec as P

HEAD_DIM = 64
STATE = 256
CONV = 4
HEADS = 8
BLOCK = 256
ROWS = 512
COLS = HEADS * HEAD_DIM
BLOCKS = ROWS // BLOCK
HALO = 16
LANES = 128
META_ROWS = 8
STORE = 28

F32 = jnp.float32
BF16 = jnp.bfloat16
NN = ((1,), (0,))
NT = ((1,), (1,))
TN = ((0,), (0,))
CTX = ("y", "zl")
TP = ("x", "zh", "core")


def mul(a, b, dims):
    return lax.dot_general(a, b, (dims, ((), ())), preferred_element_type=F32)


def split2(a):
    high = a.astype(BF16)
    return high, (a - high.astype(F32)).astype(BF16)


def split3(a):
    high = a.astype(BF16)
    rest = a - high.astype(F32)
    middle = rest.astype(BF16)
    return high, middle, (rest - middle.astype(F32)).astype(BF16)


def dot3(a, b, dims):
    return mul(a[0], b[0], dims) + (mul(a[0], b[1], dims) + mul(a[1], b[0], dims))


def exact_left(ones, b, dims):
    parts = split3(b)
    return mul(ones, parts[0], dims) + (mul(ones, parts[1], dims) + mul(ones, parts[2], dims))


def exact_right(a, ones, dims):
    parts = split3(a)
    return mul(parts[0], ones, dims) + (mul(parts[1], ones, dims) + mul(parts[2], ones, dims))


def expander(rows):
    head = lax.broadcasted_iota(jnp.int32, (rows, COLS), 0)
    col = lax.broadcasted_iota(jnp.int32, (rows, COLS), 1)
    return jnp.where((col >= head * HEAD_DIM) & (col < (head + 1) * HEAD_DIM), 1.0, 0.0).astype(BF16)


def row_col(shape=(BLOCK, BLOCK)):
    return (
        lax.broadcasted_iota(jnp.int32, shape, 0),
        lax.broadcasted_iota(jnp.int32, shape, 1),
    )


def begin(sems, *pairs, first=0):
    copies = [pltpu.make_async_copy(a, b, sems.at[first + i]) for i, (a, b) in enumerate(pairs)]
    for copy in copies:
        copy.start()
    return copies


def finish(copies):
    for copy in copies:
        copy.wait()


def sigmoid(v):
    return 1.0 / (1.0 + jnp.exp(-v))


def conv(buf, prev, rows, taps):
    buf[0:8] = prev[HALO - 8 :].astype(F32)
    buf[8 : 8 + ROWS] = rows[...].astype(F32)
    pre = taps[0:1] * buf[5 : 5 + ROWS]
    for k in range(1, CONV):
        pre = pre + taps[k : k + 1] * buf[5 + k : 5 + k + ROWS]
    return pre


def group_conv(buf, prev, gathered, taps):
    cores, pairs, own, _ = gathered.shape
    buf[0:8] = prev[HALO - 8 :].astype(F32)
    for pair in range(pairs):
        for core in range(cores):
            at = 8 + (pair * cores + core) * own
            buf[at : at + own] = gathered[core, pair].astype(F32)
    pre = taps[0:1] * buf[5 : 5 + ROWS]
    for k in range(1, CONV):
        pre = pre + taps[k : k + 1] * buf[5 + k : 5 + k + ROWS]
    return pre


def fan_kernel(rows_hbm, out_ref, sems):
    groups = rows_hbm.shape[1] // (2 * STATE)
    fan = out_ref.shape[0] // groups
    copies = []
    for owner in range(out_ref.shape[0]):
        at = owner // fan * (2 * STATE)
        copies += begin(sems, (rows_hbm.at[:, at : at + 2 * STATE], out_ref.at[owner]), first=owner)
    finish(copies)


def fold_kernel(parts_ref, out_ref):
    groups = out_ref.shape[1] // (2 * STATE)
    fan = parts_ref.shape[0] // groups
    for group in range(groups):
        total = parts_ref[group * fan]
        for one in range(1, fan):
            total = total + parts_ref[group * fan + one]
        out_ref[:, group * 2 * STATE : (group + 1) * 2 * STATE] = total


def widen(values, spread):
    return exact_right(values, spread, NN)


def widen_row(row, spread):
    return widen(jnp.broadcast_to(row, (8, LANES)), spread)[0:1]


def head_sums(values, spread):
    high, low = split2(values)
    return mul(high, spread, NT) + mul(low, spread, NT)


def feature_kernel(x_ref, prev_ref, taps_ref, log_ref, grad_ref,
                   store, xf_hi, xf_lo, ge_hi, ge_lo, cum_ref, cumt_ref, buf, act_ref, slope_ref, sems):
    pre = conv(buf, prev_ref, x_ref, taps_ref)
    gate = sigmoid(pre)
    act = pre * gate
    act_ref[...] = act
    slope_ref[...] = gate * (1.0 + pre * (1.0 - gate))
    leaving = begin(sems, (act_ref, store.at[0]), (slope_ref, store.at[1]))
    row, col = row_col()
    upper = jnp.where(row <= col, 1.0, 0.0).astype(BF16)
    lower = jnp.where(col <= row, 1.0, 0.0).astype(BF16)
    spread = expander(LANES)
    cums = []
    for b in range(BLOCKS):
        part = slice(b * BLOCK, (b + 1) * BLOCK)
        logs = log_ref[:, part]
        padded = jnp.concatenate([logs, jnp.zeros((LANES - HEADS, BLOCK), F32)], axis=0)
        cums.append(exact_left(lower, padded, NT))
        cum_ref[part] = cums[b]
        cumt_ref[b] = exact_right(logs, upper, NN)
    lasts = [cum[BLOCK - 1 : BLOCK] for cum in cums]
    for b in range(BLOCKS):
        part = slice(b * BLOCK, (b + 1) * BLOCK)
        since = cums[b] + sum(lasts[:b], jnp.zeros((1, LANES), F32))
        until = lasts[b] - cums[b] + sum(lasts[b + 1 :], jnp.zeros((1, LANES), F32))
        xf_hi[part], xf_lo[part] = split2(act[part] * widen(jnp.exp(until), spread))
        ge_hi[part], ge_lo[part] = split2(grad_ref[part].astype(F32) * widen(jnp.exp(since), spread))
    finish(leaving)


def chunk_fade(cum_ref, rows, spread):
    parts = []
    for b in range(-(-rows // BLOCK)):
        until = -cum_ref[b * BLOCK : min((b + 1) * BLOCK, rows)]
        for later in range(b, BLOCKS):
            until = until + cum_ref[(later + 1) * BLOCK - 1 : (later + 1) * BLOCK]
        parts.append(widen(jnp.exp(until), spread))
    return parts[0] if len(parts) == 1 else jnp.concatenate(parts, axis=0)


def power_scale(values):
    top = jnp.max(jnp.max(jnp.abs(values), axis=1, keepdims=True), axis=0, keepdims=True)
    return jnp.clip(14.0 - jnp.ceil(jnp.log2(jnp.maximum(top, 1e-30))), -100.0, 100.0)


def pack_piece(first, second, out, place, logs):
    count = first.shape[0]
    start = place * piece_rows(count)
    ups = [power_scale(first), power_scale(second)]
    for which, array in enumerate((first, second)):
        scaled = array * jnp.exp2(ups[which])
        for t in range(COLS // LANES):
            at = start + (which * (COLS // LANES) + t) * count
            out[at : at + count] = scaled[:, t * LANES : (t + 1) * LANES]
    lane = lax.broadcasted_iota(jnp.int32, (META_ROWS, LANES), 1)
    meta = jnp.where(lane == 16, ups[0], jnp.where(lane == 17, ups[1], 0.0))
    out[start + piece_rows(count) - META_ROWS : start + piece_rows(count)] = jnp.where(lane < 16, logs, meta)


def piece_rows(count):
    return 2 * count * (COLS // LANES) + META_ROWS


def unpack_piece(got, place, count, which):
    start = place * piece_rows(count)
    meta = got[start + piece_rows(count) - META_ROWS : start + piece_rows(count)]
    down = jnp.exp2(-meta[0:1, 16 + which : 17 + which])
    first = start + which * (COLS // LANES) * count
    return [got[first + t * count : first + (t + 1) * count] * down for t in range(COLS // LANES)]


def state_kernel(places, bc_ref, prev_ref, taps_ref, xf_hi, xf_lo, ge_hi, ge_lo, cum_ref, pack_ref, buf):
    pre = group_conv(buf, prev_ref, bc_ref, taps_ref)
    act = pre * sigmoid(pre)
    keys = split2(act[:, 0:STATE])
    queries = split2(act[:, STATE:])
    state = dot3(keys, (xf_hi[...], xf_lo[...]), TN)
    grad = dot3(queries, (ge_hi[...], ge_lo[...]), TN)
    total = jnp.zeros((1, LANES), F32)
    for b in range(BLOCKS):
        total = total + cum_ref[(b + 1) * BLOCK - 1 : (b + 1) * BLOCK]
    high = total.astype(BF16).astype(F32)
    lane = lax.broadcasted_iota(jnp.int32, (1, LANES), 1)
    logs = jnp.where(lane < 8, high, pltpu.roll(total - high, 8, 1))
    count = STATE // places
    for p in range(places):
        rows = slice(p * count, (p + 1) * count)
        pack_piece(state[rows], grad[rows], pack_ref, p, logs)


def scan_kernel(places, got_ref, out_ref):
    count = STATE // places
    spread = expander(LANES)
    lane = lax.broadcasted_iota(jnp.int32, (META_ROWS, LANES), 1)
    tiles = COLS // LANES
    decays = []
    for p in range(places):
        end = (p + 1) * piece_rows(count)
        meta = got_ref[end - META_ROWS : end]
        logs = meta + pltpu.roll(meta, LANES - 8, 1)
        decay = jnp.where(lane < 8, jnp.exp(jnp.minimum(logs, 0.0)), 0.0)
        decays.append(widen(decay, spread)[0:1])
    coming = jnp.zeros((count, COLS), F32)
    befores = []
    for p in range(places):
        befores.append(coming)
        coming = decays[p] * coming + jnp.concatenate(unpack_piece(got_ref, p, count, 0), axis=1)
    going = jnp.zeros((count, COLS), F32)
    for p in reversed(range(places)):
        pack_piece(befores[p], going, out_ref, p, 0.0)
        going = decays[p] * going + jnp.concatenate(unpack_piece(got_ref, p, count, 1), axis=1)


def block_kernel(features, grad_ref, bc_ref, prev_ref, taps_ref, cum_ref, cumt_ref, store,
                 act_ref, dx_ref, dbc_ref, slope_ref, bc_act, dlog_ref, bc_hi, bc_lo, buf, sems):
    coming = begin(sems, (features.at[0], act_ref))
    pre = group_conv(buf, prev_ref, bc_ref, taps_ref)
    gate = sigmoid(pre)
    slope_ref[...] = gate * (1.0 + pre * (1.0 - gate))
    bc_act[...] = pre * gate
    leaving = begin(sems, (slope_ref, store.at[2]), (bc_act, store.at[3]), first=1)
    bc_hi[...], bc_lo[...] = split2(bc_act[...])
    finish(coming)
    row, col = row_col()
    causal = row <= col
    later = jnp.where(col >= row, 1.0, 0.0).astype(BF16)
    before = jnp.where(col < row, 1.0, 0.0).astype(BF16)
    spread = expander(LANES)
    for b in range(BLOCKS):
        part = slice(b * BLOCK, (b + 1) * BLOCK)
        keys = (bc_hi[part, 0:STATE], bc_lo[part, 0:STATE])
        queries = (bc_hi[part, STATE:], bc_lo[part, STATE:])
        scores = dot3(keys, queries, NT)
        total = jnp.zeros((BLOCK, BLOCK), F32)
        across, down = [], []
        for h in range(HEADS):
            cols = slice(h * HEAD_DIM, (h + 1) * HEAD_DIM)
            gap = cumt_ref[b, h : h + 1, :] - cum_ref[part, h : h + 1]
            mixing = jnp.where(causal, jnp.exp(jnp.where(causal, gap, 0.0)), 0.0)
            grads = grad_ref[part, cols]
            values = split2(act_ref[part, cols])
            pairs = mixing * (mul(values[0], grads, NT) + mul(values[1], grads, NT))
            total = total + pairs
            weights = pairs * scores
            across.append(jnp.sum(weights, axis=0, keepdims=True))
            down.append(jnp.sum(weights, axis=1, keepdims=True))
            mixed = split2(mixing * scores)
            dx_ref[part, cols] = mul(mixed[0], grads, NN) + mul(mixed[1], grads, NN)
        pairs = split2(total)
        dbc_ref[part, 0:STATE] = dot3(pairs, queries, NN)
        dbc_ref[part, STATE:] = dot3(pairs, keys, TN)
        dlog_ref[part, 0:HEADS] = exact_left(later, jnp.concatenate(across, axis=0), NT) - exact_left(
            later, jnp.concatenate(down, axis=1), NN
        )
    first, second = slice(0, BLOCK), slice(BLOCK, 2 * BLOCK)
    last = cum_ref[BLOCK - 1 : BLOCK]
    fade = widen(jnp.exp(last - cum_ref[first]), spread)
    faded = act_ref[first] * fade
    grown = grad_ref[second].astype(F32) * widen(jnp.exp(cum_ref[second]), spread)
    faded2, grown2 = split2(faded), split2(grown)
    keys = (bc_hi[first, 0:STATE], bc_lo[first, 0:STATE])
    queries = (bc_hi[second, STATE:], bc_lo[second, STATE:])
    scores = split2(dot3(keys, queries, NT))
    pairs = split2(dot3(faded2, grown2, NT))
    dbc_ref[first, 0:STATE] += dot3(pairs, queries, NN)
    dbc_ref[second, STATE:] += dot3(pairs, keys, TN)
    pulls = dot3(scores, grown2, NN)
    reads = dot3(scores, faded2, TN)
    dx_ref[first] += fade * pulls
    dlog_ref[first, 0:HEADS] += exact_left(before, head_sums(faded * pulls, spread), NN)[:, 0:HEADS]
    dlog_ref[second, 0:HEADS] += exact_left(later, head_sums(grown * reads, spread), NN)[:, 0:HEADS]
    leaving += begin(
        sems, (dx_ref, store.at[0]), (dbc_ref, store.at[1]), (dlog_ref, store.at[4, :, 0:LANES]), first=3
    )
    finish(leaving)


def unpack_states(places, got_ref, which, out):
    count = STATE // places
    for p in range(places):
        for t, tile in enumerate(unpack_piece(got_ref, p, count, which)):
            out[p * count : (p + 1) * count, t * LANES : (t + 1) * LANES] = tile


def open_kernel(places, got_ref, xf_hi, xf_lo, ge_hi, ge_lo, cum_ref, features, blocks,
                store, both_ref, halo_ref, coming, going, states, dx, dbc, slope, bc_act, xslope, sems):
    top = slice(0, HALO)
    arriving = begin(
        sems, (blocks.at[0, top], dx), (blocks.at[1, top], dbc), (blocks.at[2, top], slope),
        (blocks.at[3, top], bc_act), (features.at[1, top], xslope),
    )
    unpack_states(places, got_ref, 0, coming)
    unpack_states(places, got_ref, 1, going)
    enter = split2(coming[...])
    leave = split2(going[...])
    states[0, 0:STATE], states[0, STATE:] = enter
    states[1, 0:STATE], states[1, STATE:] = leave
    leaving = begin(sems, (states, store.at[0:2]), first=5)
    both_ref[...] = jnp.broadcast_to(jnp.sum(coming[...] * going[...], axis=0, keepdims=True), (8, COLS))
    fade = chunk_fade(cum_ref, HALO, expander(LANES))
    finish(arriving)
    pulls = dot3(split2(bc_act[:, 0:STATE]), leave, NN)
    keys = dbc[:, 0:STATE] + dot3((xf_hi[top], xf_lo[top]), leave, NT)
    queries = dbc[:, STATE:] + dot3((ge_hi[top], ge_lo[top]), enter, NT)
    gx = (dx[...] + fade * pulls) * xslope[...]
    halo_ref[:, 0:COLS] = gx[0:8]
    halo_ref[:, COLS : COLS + STATE] = (keys * slope[:, 0:STATE])[0:8]
    halo_ref[:, COLS + STATE :] = (queries * slope[:, STATE:])[0:8]
    finish(leaving)


def group_kernel(xf_hi, xf_lo, ge_hi, ge_lo, blocks, store, gbc_ref, states, dbc_ref, slope_ref, sems):
    first = begin(sems, (store.at[0:2], states))
    arriving = begin(sems, (blocks.at[1], dbc_ref), (blocks.at[2], slope_ref), first=1)
    finish(first)
    keys = dot3((xf_hi[...], xf_lo[...]), (states[1, 0:STATE], states[1, STATE:]), NT)
    queries = dot3((ge_hi[...], ge_lo[...]), (states[0, 0:STATE], states[0, STATE:]), NT)
    finish(arriving)
    gbc_ref[:, 0:STATE] = (dbc_ref[:, 0:STATE] + keys) * slope_ref[:, 0:STATE]
    gbc_ref[:, STATE:] = (dbc_ref[:, STATE:] + queries) * slope_ref[:, STATE:]


def back_conv(buf, taps):
    out = taps[0:1] * buf[3 : 3 + ROWS]
    for k in range(1, CONV):
        out = out + taps[k : k + 1] * buf[3 - k : 3 - k + ROWS]
    return out


def grad_bc_kernel(own, core_ref, rows_ref, halo_ref, taps_ref, keep_ref, give_ref, buf, terms):
    buf[0:ROWS] = rows_ref[...]
    buf[ROWS : ROWS + 8] = halo_ref[:, COLS:]
    terms[...] = back_conv(buf, taps_ref)
    core = core_ref[0]
    for pair in range(ROWS // (2 * own)):
        at = pair * 2 * own
        keep_ref[pair] = terms[pl.ds(pl.multiple_of(at + core * own, own), own)]
        give_ref[pair] = terms[pl.ds(pl.multiple_of(at + (1 - core) * own, own), own)]


def carry_kernel(xf_hi, xf_lo, ge_hi, ge_lo, cum_ref, features, blocks, store, both_ref, halo_ref, taps_ref,
                 grad_ref, glog_ref, buf, states, bc_act, dx_ref, xslope_ref, dlog_ref, sems):
    arriving = begin(
        sems, (store.at[0:2], states), (blocks.at[3], bc_act), (blocks.at[0], dx_ref),
        (features.at[1], xslope_ref), (blocks.at[4, :, 0:LANES], dlog_ref),
    )
    spread = expander(LANES)
    fade = chunk_fade(cum_ref, ROWS, spread)
    finish(arriving)
    pulls = dot3(split2(bc_act[:, 0:STATE]), (states[1, 0:STATE], states[1, STATE:]), NN)
    buf[0:ROWS] = (dx_ref[...] + fade * pulls) * xslope_ref[...]
    buf[ROWS : ROWS + 8] = halo_ref[:, 0:COLS]
    grad_ref[...] = back_conv(buf, taps_ref).astype(BF16)
    reads = dot3(split2(bc_act[:, STATE:]), (states[0, 0:STATE], states[0, STATE:]), NN)
    grown = ge_hi[...].astype(F32) + ge_lo[...].astype(F32)
    faded = xf_hi[...].astype(F32) + xf_lo[...].astype(F32)
    across = head_sums(grown * reads, spread)
    down = head_sums(faded * pulls, spread)
    last = jnp.zeros((1, LANES), F32)
    for b in range(BLOCKS):
        last = last + cum_ref[(b + 1) * BLOCK - 1 : (b + 1) * BLOCK]
    both = head_sums(both_ref[...], spread)[0:1] * jnp.exp(last)
    row, col = row_col((ROWS, ROWS))
    later = jnp.where(col >= row, 1.0, 0.0).astype(BF16)
    before = jnp.where(col < row, 1.0, 0.0).astype(BF16)
    found = dlog_ref[...] + exact_left(later, across, NN) + exact_left(before, down, NN) + both
    glog_ref[...] = jnp.transpose(found)[0:HEADS]


def call(kernel, outs, scratch=(), hbm_in=(), hbm_out=(), smem=(), count=0, sems=0, vmem=40, flops=1 << 26, size=1 << 22):
    def place(i, far):
        return pl.BlockSpec(memory_space=pltpu.SMEM if i in smem else pltpu.HBM if i in far else pltpu.VMEM)

    return pl.pallas_call(
        kernel,
        out_shape=[jax.ShapeDtypeStruct(shape, dtype) for shape, dtype in outs],
        in_specs=[place(i, hbm_in) for i in range(count)],
        out_specs=[
            pl.BlockSpec(memory_space=pltpu.HBM if i in hbm_out else pltpu.VMEM) for i in range(len(outs))
        ],
        scratch_shapes=[pltpu.VMEM(shape, dtype) for shape, dtype in scratch]
        + ([pltpu.SemaphoreType.DMA((sems,))] if sems else []),
        compiler_params=pltpu.CompilerParams(vmem_limit_bytes=vmem * 2**20),
        cost_estimate=pl.CostEstimate(flops=flops, bytes_accessed=size, transcendentals=0),
    )


def shifted(array, by):
    devices = lax.axis_size(CTX)
    pairs = [(i, i + by) for i in range(devices) if 0 <= i + by < devices]
    return lax.ppermute(array, CTX, pairs)


def per_device(x_in, bc_in, conv_x, conv_bc, log_decay, grad_y):
    core = lax.axis_index("core")
    owners = lax.axis_size(("x", "zh"))
    places = lax.axis_size(CTX)
    groups = bc_in.shape[1] // (2 * STATE)
    own = bc_in.shape[0]
    fan = owners // groups
    group = lax.axis_index(("x", "zh")) // fan
    taps_bc = lax.dynamic_slice_in_dim(conv_bc, group * (2 * STATE), 2 * STATE, 1)
    swap = [(0, 1), (1, 0)]

    (spread,) = call(
        fan_kernel, [((owners, own, 2 * STATE), BF16)], hbm_in=(0,), count=1, sems=owners, vmem=62
    )(bc_in)
    mine = lax.all_to_all(spread, ("x", "zh"), 0, 0, tiled=True)
    x_prev = shifted(x_in[ROWS - HALO :], 1)
    wide = (ROWS, COLS)
    padded = ((ROWS + 8, COLS), F32)
    store = (STORE,) + wide
    made = call(
        feature_kernel,
        [(store, F32)] + [(wide, BF16)] * 4 + [((ROWS, LANES), F32), ((BLOCKS, 8, BLOCK), F32)],
        [padded, (wide, F32), (wide, F32)], hbm_out=(0,), count=5, sems=2,
    )(x_in, x_prev, conv_x, log_decay.T, grad_y)
    mine, made = lax.optimization_barrier((mine, made))
    features, xf_hi, xf_lo, ge_hi, ge_lo, cum, cumt = made
    scaled = (xf_hi, xf_lo, ge_hi, ge_lo)
    bc_rows = lax.all_gather(mine, "core")
    bc_prev = shifted(bc_rows[1, owners - 1], 1)
    packed = (places * piece_rows(STATE // places), LANES)
    (sent,) = call(functools.partial(state_kernel, places), [(packed, F32)], [padded], count=8)(
        bc_rows, bc_prev, taps_bc, *scaled, cum
    )
    got = lax.all_to_all(sent.astype(jnp.float16), CTX, 0, 0, tiled=True)
    (blocks,) = call(
        block_kernel, [(store, F32)],
        [(wide, F32)] * 5 + [((ROWS, LANES), F32)] + [(wide, BF16)] * 2 + [padded],
        hbm_in=(0,), hbm_out=(0,), count=7, sems=6,
    )(features, grad_y, bc_rows, bc_prev, taps_bc, cum, cumt)

    (back,) = call(functools.partial(scan_kernel, places), [(packed, F32)], count=1)(got.astype(F32))
    carried = lax.all_to_all(back.astype(jnp.float16), CTX, 0, 0, tiled=True).astype(F32)

    half = (STATE, COLS)
    top = (HALO, COLS)
    pair = ((2,) + wide, BF16)
    states, both, first = call(
        functools.partial(open_kernel, places),
        [((2 * STORE,) + wide, BF16), ((8, COLS), F32), ((8, COLS + 2 * STATE), F32)],
        [(half, F32)] * 2 + [pair] + [(top, F32)] * 5,
        hbm_in=(6, 7), hbm_out=(0,), count=8, sems=6,
    )(carried, *scaled, cum, features, blocks)
    halo = shifted(first, -1)
    (gbc,) = call(
        group_kernel, [(wide, F32)], [pair] + [(wide, F32)] * 2, hbm_in=(4, 5), count=6, sems=3
    )(*scaled, blocks, states)
    piece = (owners, own, 2 * STATE)
    keep, give = call(
        functools.partial(grad_bc_kernel, own), [(piece, F32)] * 2, [padded, (wide, F32)], smem=(0,), count=4
    )(core.reshape(1), gbc, halo, taps_bc)
    summed = keep + lax.ppermute(give, "core", swap)
    parts = lax.all_to_all(summed, ("x", "zh"), 0, 0, tiled=True)
    grad_x, glog = call(
        carry_kernel,
        [(wide, BF16), ((HEADS, ROWS), F32)],
        [padded, pair] + [(wide, F32)] * 3 + [((ROWS, LANES), F32)],
        hbm_in=(5, 6, 7), count=11, sems=5,
    )(*scaled, cum, features, blocks, states, both, halo, conv_x)
    (grad_bc,) = call(fold_kernel, [((own, groups * 2 * STATE), F32)], count=1)(parts)
    return grad_x, grad_bc, glog.T


def solution(mesh):
    fine = Mesh(mesh.devices.reshape(8, 2, 4, 4, 2), CTX + TP)
    return jax.shard_map(
        per_device,
        mesh=fine,
        in_specs=(P(CTX, TP), P(CTX + TP, None), P(None, TP), P(), P(CTX, TP), P(CTX, TP)),
        out_specs=(P(CTX, TP), P(CTX + TP, None), P(CTX, TP)),
        check_vma=False,
    )
```

```python
import functools

import jax
import jax.numpy as jnp
from jax import lax
from jax.experimental import pallas as pl
from jax.experimental.pallas import tpu as pltpu
from jax.sharding import Mesh, PartitionSpec as P

HEAD_DIM = 64
STATE = 256
CONV = 4
HEADS = 8
BLOCK = 256
ROWS = 512
COLS = HEADS * HEAD_DIM
BLOCKS = ROWS // BLOCK
HALO = 16
LANES = 128
META_ROWS = 8
STORE = 28

F32 = jnp.float32
BF16 = jnp.bfloat16
NN = ((1,), (0,))
NT = ((1,), (1,))
TN = ((0,), (0,))
CTX = ("y", "zl")
TP = ("x", "zh", "core")


def mul(a, b, dims):
    return lax.dot_general(a, b, (dims, ((), ())), preferred_element_type=F32)


def split2(a):
    high = a.astype(BF16)
    return high, (a - high.astype(F32)).astype(BF16)


def split3(a):
    high = a.astype(BF16)
    rest = a - high.astype(F32)
    middle = rest.astype(BF16)
    return high, middle, (rest - middle.astype(F32)).astype(BF16)


def dot3(a, b, dims):
    return mul(a[0], b[0], dims) + (mul(a[0], b[1], dims) + mul(a[1], b[0], dims))


def exact_left(ones, b, dims):
    parts = split3(b)
    return mul(ones, parts[0], dims) + (mul(ones, parts[1], dims) + mul(ones, parts[2], dims))


def exact_right(a, ones, dims):
    parts = split3(a)
    return mul(parts[0], ones, dims) + (mul(parts[1], ones, dims) + mul(parts[2], ones, dims))


def expander(rows):
    head = lax.broadcasted_iota(jnp.int32, (rows, COLS), 0)
    col = lax.broadcasted_iota(jnp.int32, (rows, COLS), 1)
    return jnp.where((col >= head * HEAD_DIM) & (col < (head + 1) * HEAD_DIM), 1.0, 0.0).astype(BF16)


def row_col(shape=(BLOCK, BLOCK)):
    return (
        lax.broadcasted_iota(jnp.int32, shape, 0),
        lax.broadcasted_iota(jnp.int32, shape, 1),
    )


def begin(sems, *pairs, first=0):
    copies = [pltpu.make_async_copy(a, b, sems.at[first + i]) for i, (a, b) in enumerate(pairs)]
    for copy in copies:
        copy.start()
    return copies


def finish(copies):
    for copy in copies:
        copy.wait()


def sigmoid(v):
    return 1.0 / (1.0 + jnp.exp(-v))


def conv(buf, prev, rows, taps):
    buf[0:8] = prev[HALO - 8 :].astype(F32)
    buf[8 : 8 + ROWS] = rows[...].astype(F32)
    pre = taps[0:1] * buf[5 : 5 + ROWS]
    for k in range(1, CONV):
        pre = pre + taps[k : k + 1] * buf[5 + k : 5 + k + ROWS]
    return pre


def group_conv(buf, prev, gathered, taps):
    cores, pairs, own, _ = gathered.shape
    buf[0:8] = prev[0][HALO - 8 :].astype(F32) + prev[1][HALO - 8 :].astype(F32)
    for pair in range(pairs):
        for core in range(cores):
            at = 8 + (pair * cores + core) * own
            buf[at : at + own] = gathered[core, pair].astype(F32)
    pre = taps[0:1] * buf[5 : 5 + ROWS]
    for k in range(1, CONV):
        pre = pre + taps[k : k + 1] * buf[5 + k : 5 + k + ROWS]
    return pre


def fan_kernel(rows_hbm, out_ref, sems):
    groups = rows_hbm.shape[1] // (2 * STATE)
    fan = out_ref.shape[0] // groups
    copies = []
    for owner in range(out_ref.shape[0]):
        at = owner // fan * (2 * STATE)
        copies += begin(sems, (rows_hbm.at[:, at : at + 2 * STATE], out_ref.at[owner]), first=owner)
    finish(copies)


def widen(values, spread):
    return exact_right(values, spread, NN)


def widen_row(row, spread):
    return widen(jnp.broadcast_to(row, (8, LANES)), spread)[0:1]


def head_sums(values, spread):
    high, low = split2(values)
    return mul(high, spread, NT) + mul(low, spread, NT)


def decay_kernel(log_ref, grad_ref, ge_hi, ge_lo, cum_ref, cumt_ref):
    row, col = row_col()
    upper = jnp.where(row <= col, 1.0, 0.0).astype(BF16)
    lower = jnp.where(col <= row, 1.0, 0.0).astype(BF16)
    spread = expander(LANES)
    before = jnp.zeros((1, LANES), F32)
    for b in range(BLOCKS):
        part = slice(b * BLOCK, (b + 1) * BLOCK)
        logs = log_ref[:, part]
        padded = jnp.concatenate([logs, jnp.zeros((LANES - HEADS, BLOCK), F32)], axis=0)
        cum = exact_left(lower, padded, NT)
        cum_ref[part] = cum
        cumt_ref[b] = exact_right(logs, upper, NN)
        ge_hi[part], ge_lo[part] = split2(grad_ref[part].astype(F32) * widen(jnp.exp(before + cum), spread))
        before = before + cum[BLOCK - 1 : BLOCK]


def feature_kernel(x_ref, prev_ref, taps_ref, cum_ref, store, xf_hi, xf_lo, buf, act_ref, slope_ref, sems):
    pre = conv(buf, prev_ref, x_ref, taps_ref)
    gate = sigmoid(pre)
    act = pre * gate
    act_ref[...] = act
    slope_ref[...] = gate * (1.0 + pre * (1.0 - gate))
    leaving = begin(sems, (act_ref, store.at[0]), (slope_ref, store.at[1]))
    xf_hi[...], xf_lo[...] = split2(act * chunk_fade(cum_ref, ROWS, expander(LANES)))
    finish(leaving)


def chunk_fade(cum_ref, rows, spread):
    parts = []
    for b in range(-(-rows // BLOCK)):
        until = -cum_ref[b * BLOCK : min((b + 1) * BLOCK, rows)]
        for later in range(b, BLOCKS):
            until = until + cum_ref[(later + 1) * BLOCK - 1 : (later + 1) * BLOCK]
        parts.append(widen(jnp.exp(until), spread))
    return parts[0] if len(parts) == 1 else jnp.concatenate(parts, axis=0)


def power_scale(values):
    top = jnp.max(jnp.max(jnp.abs(values), axis=1, keepdims=True), axis=0, keepdims=True)
    return jnp.clip(14.0 - jnp.ceil(jnp.log2(jnp.maximum(top, 1e-30))), -100.0, 100.0)


def pack_piece(first, second, out, place, logs):
    count = first.shape[0]
    start = place * piece_rows(count)
    ups = [power_scale(first), power_scale(second)]
    for which, array in enumerate((first, second)):
        scaled = array * jnp.exp2(ups[which])
        for t in range(COLS // LANES):
            at = start + (which * (COLS // LANES) + t) * count
            out[at : at + count] = scaled[:, t * LANES : (t + 1) * LANES]
    lane = lax.broadcasted_iota(jnp.int32, (META_ROWS, LANES), 1)
    meta = jnp.where(lane == 16, ups[0], jnp.where(lane == 17, ups[1], 0.0))
    out[start + piece_rows(count) - META_ROWS : start + piece_rows(count)] = jnp.where(lane < 16, logs, meta)


def piece_rows(count):
    return 2 * count * (COLS // LANES) + META_ROWS


def unpack_piece(got, place, count, which):
    start = place * piece_rows(count)
    meta = got[start + piece_rows(count) - META_ROWS : start + piece_rows(count)]
    down = jnp.exp2(-meta[0:1, 16 + which : 17 + which])
    first = start + which * (COLS // LANES) * count
    return [got[first + t * count : first + (t + 1) * count] * down for t in range(COLS // LANES)]


def state_kernel(places, bc_ref, prev_0, prev_1, taps_ref, xf_hi, xf_lo, ge_hi, ge_lo, cum_ref, pack_ref, buf):
    pre = group_conv(buf, (prev_0, prev_1), bc_ref, taps_ref)
    act = pre * sigmoid(pre)
    keys = split2(act[:, 0:STATE])
    queries = split2(act[:, STATE:])
    state = dot3(keys, (xf_hi[...], xf_lo[...]), TN)
    grad = dot3(queries, (ge_hi[...], ge_lo[...]), TN)
    total = jnp.zeros((1, LANES), F32)
    for b in range(BLOCKS):
        total = total + cum_ref[(b + 1) * BLOCK - 1 : (b + 1) * BLOCK]
    high = total.astype(BF16).astype(F32)
    lane = lax.broadcasted_iota(jnp.int32, (1, LANES), 1)
    logs = jnp.where(lane < 8, high, pltpu.roll(total - high, 8, 1))
    count = STATE // places
    for p in range(places):
        rows = slice(p * count, (p + 1) * count)
        pack_piece(state[rows], grad[rows], pack_ref, p, logs)


def term_rows(own):
    return own * (2 * STATE // LANES) + META_ROWS


def sum_kernel(keep_ref, got_ref, out_ref):
    own = keep_ref.shape[1]
    for owner in range(keep_ref.shape[0]):
        start = owner * term_rows(own)
        terms = keep_ref[owner] + got_ref[owner]
        up = power_scale(terms)
        scaled = terms * jnp.exp2(up)
        for t in range(2 * STATE // LANES):
            out_ref[start + t * own : start + (t + 1) * own] = scaled[:, t * LANES : (t + 1) * LANES]
        end = start + term_rows(own)
        out_ref[end - META_ROWS : end] = jnp.broadcast_to(up, (META_ROWS, LANES))


def fold_kernel(parts_ref, out_ref):
    own = out_ref.shape[0]
    groups = out_ref.shape[1] // (2 * STATE)
    fan = parts_ref.shape[0] // term_rows(own) // groups
    for group in range(groups):
        downs = []
        for one in range(fan):
            end = (group * fan + one + 1) * term_rows(own)
            downs.append(jnp.exp2(-parts_ref[end - META_ROWS : end - META_ROWS + 1]))
        for t in range(2 * STATE // LANES):
            total = jnp.zeros((own, LANES), F32)
            for one in range(fan):
                start = (group * fan + one) * term_rows(own) + t * own
                total = total + parts_ref[start : start + own] * downs[one]
            at = group * 2 * STATE + t * LANES
            out_ref[:, at : at + LANES] = total


def scan_kernel(places, got_ref, out_ref):
    count = STATE // places
    spread = expander(LANES)
    lane = lax.broadcasted_iota(jnp.int32, (META_ROWS, LANES), 1)
    tiles = COLS // LANES
    decays = []
    for p in range(places):
        end = (p + 1) * piece_rows(count)
        meta = got_ref[end - META_ROWS : end]
        logs = meta + pltpu.roll(meta, LANES - 8, 1)
        decay = jnp.where(lane < 8, jnp.exp(jnp.minimum(logs, 0.0)), 0.0)
        decays.append(widen(decay, spread)[0:1])
    coming = jnp.zeros((count, COLS), F32)
    befores = []
    for p in range(places):
        befores.append(coming)
        coming = decays[p] * coming + jnp.concatenate(unpack_piece(got_ref, p, count, 0), axis=1)
    going = jnp.zeros((count, COLS), F32)
    for p in reversed(range(places)):
        pack_piece(befores[p], going, out_ref, p, 0.0)
        going = decays[p] * going + jnp.concatenate(unpack_piece(got_ref, p, count, 1), axis=1)


def block_kernel(features, grad_ref, bc_ref, prev_0, prev_1, taps_ref, cum_ref, cumt_ref, store,
                 act_ref, dx_ref, dbc_ref, slope_ref, bc_act, dlog_ref, bc_hi, bc_lo, buf, sems):
    coming = begin(sems, (features.at[0], act_ref))
    pre = group_conv(buf, (prev_0, prev_1), bc_ref, taps_ref)
    gate = sigmoid(pre)
    slope_ref[...] = gate * (1.0 + pre * (1.0 - gate))
    bc_act[...] = pre * gate
    leaving = begin(sems, (slope_ref, store.at[2]), (bc_act, store.at[3]), first=1)
    bc_hi[...], bc_lo[...] = split2(bc_act[...])
    finish(coming)
    row, col = row_col()
    causal = row <= col
    later = jnp.where(col >= row, 1.0, 0.0).astype(BF16)
    before = jnp.where(col < row, 1.0, 0.0).astype(BF16)
    spread = expander(LANES)
    for b in range(BLOCKS):
        part = slice(b * BLOCK, (b + 1) * BLOCK)
        keys = (bc_hi[part, 0:STATE], bc_lo[part, 0:STATE])
        queries = (bc_hi[part, STATE:], bc_lo[part, STATE:])
        scores = dot3(keys, queries, NT)
        total = jnp.zeros((BLOCK, BLOCK), F32)
        across, down = [], []
        for h in range(HEADS):
            cols = slice(h * HEAD_DIM, (h + 1) * HEAD_DIM)
            gap = cumt_ref[b, h : h + 1, :] - cum_ref[part, h : h + 1]
            mixing = jnp.where(causal, jnp.exp(jnp.where(causal, gap, 0.0)), 0.0)
            grads = grad_ref[part, cols]
            values = split2(act_ref[part, cols])
            pairs = mixing * (mul(values[0], grads, NT) + mul(values[1], grads, NT))
            total = total + pairs
            weights = pairs * scores
            across.append(jnp.sum(weights, axis=0, keepdims=True))
            down.append(jnp.sum(weights, axis=1, keepdims=True))
            mixed = split2(mixing * scores)
            dx_ref[part, cols] = mul(mixed[0], grads, NN) + mul(mixed[1], grads, NN)
        pairs = split2(total)
        dbc_ref[part, 0:STATE] = dot3(pairs, queries, NN)
        dbc_ref[part, STATE:] = dot3(pairs, keys, TN)
        dlog_ref[part, 0:HEADS] = exact_left(later, jnp.concatenate(across, axis=0), NT) - exact_left(
            later, jnp.concatenate(down, axis=1), NN
        )
    first, second = slice(0, BLOCK), slice(BLOCK, 2 * BLOCK)
    last = cum_ref[BLOCK - 1 : BLOCK]
    fade = widen(jnp.exp(last - cum_ref[first]), spread)
    faded = act_ref[first] * fade
    grown = grad_ref[second].astype(F32) * widen(jnp.exp(cum_ref[second]), spread)
    faded2, grown2 = split2(faded), split2(grown)
    keys = (bc_hi[first, 0:STATE], bc_lo[first, 0:STATE])
    queries = (bc_hi[second, STATE:], bc_lo[second, STATE:])
    scores = split2(dot3(keys, queries, NT))
    pairs = split2(dot3(faded2, grown2, NT))
    dbc_ref[first, 0:STATE] += dot3(pairs, queries, NN)
    dbc_ref[second, STATE:] += dot3(pairs, keys, TN)
    pulls = dot3(scores, grown2, NN)
    reads = dot3(scores, faded2, TN)
    dx_ref[first] += fade * pulls
    dlog_ref[first, 0:HEADS] += exact_left(before, head_sums(faded * pulls, spread), NN)[:, 0:HEADS]
    dlog_ref[second, 0:HEADS] += exact_left(later, head_sums(grown * reads, spread), NN)[:, 0:HEADS]
    leaving += begin(
        sems, (dx_ref, store.at[0]), (dbc_ref, store.at[1]), (dlog_ref, store.at[4, :, 0:LANES]), first=3
    )
    finish(leaving)


def unpack_states(places, got_ref, which, out):
    count = STATE // places
    for p in range(places):
        for t, tile in enumerate(unpack_piece(got_ref, p, count, which)):
            out[p * count : (p + 1) * count, t * LANES : (t + 1) * LANES] = tile


def open_kernel(places, got_ref, xf_hi, xf_lo, ge_hi, ge_lo, cum_ref, features, blocks,
                store, both_ref, halo_ref, coming, going, states, dx, dbc, slope, bc_act, xslope, sems):
    top = slice(0, HALO)
    arriving = begin(
        sems, (blocks.at[0, top], dx), (blocks.at[1, top], dbc), (blocks.at[2, top], slope),
        (blocks.at[3, top], bc_act), (features.at[1, top], xslope),
    )
    unpack_states(places, got_ref, 0, coming)
    unpack_states(places, got_ref, 1, going)
    enter = split2(coming[...])
    leave = split2(going[...])
    states[0, 0:STATE], states[0, STATE:] = enter
    states[1, 0:STATE], states[1, STATE:] = leave
    leaving = begin(sems, (states, store.at[0:2]), first=5)
    both_ref[...] = jnp.broadcast_to(jnp.sum(coming[...] * going[...], axis=0, keepdims=True), (8, COLS))
    fade = chunk_fade(cum_ref, HALO, expander(LANES))
    finish(arriving)
    pulls = dot3(split2(bc_act[:, 0:STATE]), leave, NN)
    keys = dbc[:, 0:STATE] + dot3((xf_hi[top], xf_lo[top]), leave, NT)
    queries = dbc[:, STATE:] + dot3((ge_hi[top], ge_lo[top]), enter, NT)
    gx = (dx[...] + fade * pulls) * xslope[...]
    halo_ref[:, 0:COLS] = gx[0:8]
    halo_ref[:, COLS : COLS + STATE] = (keys * slope[:, 0:STATE])[0:8]
    halo_ref[:, COLS + STATE :] = (queries * slope[:, STATE:])[0:8]
    finish(leaving)


def group_kernel(xf_hi, xf_lo, ge_hi, ge_lo, blocks, store, gbc_ref, states, dbc_ref, slope_ref, sems):
    first = begin(sems, (store.at[0:2], states))
    arriving = begin(sems, (blocks.at[1], dbc_ref), (blocks.at[2], slope_ref), first=1)
    finish(first)
    keys = dot3((xf_hi[...], xf_lo[...]), (states[1, 0:STATE], states[1, STATE:]), NT)
    queries = dot3((ge_hi[...], ge_lo[...]), (states[0, 0:STATE], states[0, STATE:]), NT)
    finish(arriving)
    gbc_ref[:, 0:STATE] = (dbc_ref[:, 0:STATE] + keys) * slope_ref[:, 0:STATE]
    gbc_ref[:, STATE:] = (dbc_ref[:, STATE:] + queries) * slope_ref[:, STATE:]


def back_conv(buf, taps):
    out = taps[0:1] * buf[3 : 3 + ROWS]
    for k in range(1, CONV):
        out = out + taps[k : k + 1] * buf[3 - k : 3 - k + ROWS]
    return out


def grad_bc_kernel(own, core_ref, rows_ref, halo_ref, taps_ref, keep_ref, give_ref, buf, terms):
    buf[0:ROWS] = rows_ref[...]
    buf[ROWS : ROWS + 8] = halo_ref[:, COLS:]
    terms[...] = back_conv(buf, taps_ref)
    core = core_ref[0]
    for pair in range(ROWS // (2 * own)):
        at = pair * 2 * own
        keep_ref[pair] = terms[pl.ds(pl.multiple_of(at + core * own, own), own)]
        give_ref[pair] = terms[pl.ds(pl.multiple_of(at + (1 - core) * own, own), own)]


def carry_kernel(xf_hi, xf_lo, ge_hi, ge_lo, cum_ref, features, blocks, store, both_ref, halo_ref, taps_ref,
                 grad_ref, glog_ref, buf, states, bc_act, dx_ref, xslope_ref, dlog_ref, sems):
    arriving = begin(
        sems, (store.at[0:2], states), (blocks.at[3], bc_act), (blocks.at[0], dx_ref),
        (features.at[1], xslope_ref), (blocks.at[4, :, 0:LANES], dlog_ref),
    )
    spread = expander(LANES)
    fade = chunk_fade(cum_ref, ROWS, spread)
    finish(arriving)
    pulls = dot3(split2(bc_act[:, 0:STATE]), (states[1, 0:STATE], states[1, STATE:]), NN)
    buf[0:ROWS] = (dx_ref[...] + fade * pulls) * xslope_ref[...]
    buf[ROWS : ROWS + 8] = halo_ref[:, 0:COLS]
    grad_ref[...] = back_conv(buf, taps_ref).astype(BF16)
    reads = dot3(split2(bc_act[:, STATE:]), (states[0, 0:STATE], states[0, STATE:]), NN)
    grown = ge_hi[...].astype(F32) + ge_lo[...].astype(F32)
    faded = xf_hi[...].astype(F32) + xf_lo[...].astype(F32)
    across = head_sums(grown * reads, spread)
    down = head_sums(faded * pulls, spread)
    last = jnp.zeros((1, LANES), F32)
    for b in range(BLOCKS):
        last = last + cum_ref[(b + 1) * BLOCK - 1 : (b + 1) * BLOCK]
    both = head_sums(both_ref[...], spread)[0:1] * jnp.exp(last)
    row, col = row_col((ROWS, ROWS))
    later = jnp.where(col >= row, 1.0, 0.0).astype(BF16)
    before = jnp.where(col < row, 1.0, 0.0).astype(BF16)
    found = dlog_ref[...] + exact_left(later, across, NN) + exact_left(before, down, NN) + both
    glog_ref[...] = jnp.transpose(found)[0:HEADS]


def call(kernel, outs, scratch=(), hbm_in=(), hbm_out=(), smem=(), count=0, sems=0, vmem=40, flops=1 << 26, size=1 << 22):
    def place(i, far):
        return pl.BlockSpec(memory_space=pltpu.SMEM if i in smem else pltpu.HBM if i in far else pltpu.VMEM)

    return pl.pallas_call(
        kernel,
        out_shape=[jax.ShapeDtypeStruct(shape, dtype) for shape, dtype in outs],
        in_specs=[place(i, hbm_in) for i in range(count)],
        out_specs=[
            pl.BlockSpec(memory_space=pltpu.HBM if i in hbm_out else pltpu.VMEM) for i in range(len(outs))
        ],
        scratch_shapes=[pltpu.VMEM(shape, dtype) for shape, dtype in scratch]
        + ([pltpu.SemaphoreType.DMA((sems,))] if sems else []),
        compiler_params=pltpu.CompilerParams(vmem_limit_bytes=vmem * 2**20),
        cost_estimate=pl.CostEstimate(flops=flops, bytes_accessed=size, transcendentals=0),
    )


def shifted(array, by):
    devices = lax.axis_size(CTX)
    pairs = [(i, i + by) for i in range(devices) if 0 <= i + by < devices]
    return lax.ppermute(array, CTX, pairs)


def per_device(x_in, bc_in, conv_x, conv_bc, log_decay, grad_y):
    core = lax.axis_index("core")
    owners = lax.axis_size(("x", "zh"))
    places = lax.axis_size(CTX)
    groups = bc_in.shape[1] // (2 * STATE)
    own = bc_in.shape[0]
    fan = owners // groups
    group = lax.axis_index(("x", "zh")) // fan
    taps_bc = lax.dynamic_slice_in_dim(conv_bc, group * (2 * STATE), 2 * STATE, 1)
    swap = [(0, 1), (1, 0)]

    (spread,) = call(
        fan_kernel, [((owners, own, 2 * STATE), BF16)], hbm_in=(0,), count=1, sems=owners, vmem=62
    )(bc_in)
    mine = lax.all_to_all(spread, ("x", "zh"), 0, 0, tiled=True)
    x_prev = shifted(x_in[ROWS - HALO :], 1)
    wide = (ROWS, COLS)
    padded = ((ROWS + 8, COLS), F32)
    store = (STORE,) + wide
    ge_hi, ge_lo, cum, cumt = call(
        decay_kernel, [(wide, BF16)] * 2 + [((ROWS, LANES), F32), ((BLOCKS, HEADS, BLOCK), F32)], count=2
    )(log_decay.T, grad_y)
    made = call(
        feature_kernel, [(store, F32)] + [(wide, BF16)] * 2, [padded, (wide, F32), (wide, F32)],
        hbm_out=(0,), count=4, sems=2,
    )(x_in, x_prev, conv_x, cum)
    mine, made = lax.optimization_barrier((mine, made))
    features, xf_hi, xf_lo = made
    scaled = (xf_hi, xf_lo, ge_hi, ge_lo)
    bc_prev = [
        lax.ppermute(
            mine[owners - 1], CTX + ("core",), [(2 * i + 1, 2 * (i + 1) + to) for i in range(places - 1)]
        )
        for to in (0, 1)
    ]
    bc_rows = lax.all_gather(mine, "core")
    packed = (places * piece_rows(STATE // places), LANES)
    (sent,) = call(functools.partial(state_kernel, places), [(packed, F32)], [padded], count=9)(
        bc_rows, *bc_prev, taps_bc, *scaled, cum
    )
    got = lax.all_to_all(sent.astype(jnp.float16), CTX, 0, 0, tiled=True)
    (blocks,) = call(
        block_kernel, [(store, F32)],
        [(wide, F32)] * 5 + [((ROWS, LANES), F32)] + [(wide, BF16)] * 2 + [padded],
        hbm_in=(0,), hbm_out=(0,), count=8, sems=6,
    )(features, grad_y, bc_rows, *bc_prev, taps_bc, cum, cumt)

    (back,) = call(functools.partial(scan_kernel, places), [(packed, F32)], count=1)(got.astype(F32))
    carried = lax.all_to_all(back.astype(jnp.float16), CTX, 0, 0, tiled=True).astype(F32)

    half = (STATE, COLS)
    top = (HALO, COLS)
    pair = ((2,) + wide, BF16)
    states, both, first = call(
        functools.partial(open_kernel, places),
        [((2 * STORE,) + wide, BF16), ((8, COLS), F32), ((8, COLS + 2 * STATE), F32)],
        [(half, F32)] * 2 + [pair] + [(top, F32)] * 5,
        hbm_in=(6, 7), hbm_out=(0,), count=8, sems=6,
    )(carried, *scaled, cum, features, blocks)
    halo = shifted(first, -1)
    (gbc,) = call(
        group_kernel, [(wide, F32)], [pair] + [(wide, F32)] * 2, hbm_in=(4, 5), count=6, sems=3
    )(*scaled, blocks, states)
    piece = (owners, own, 2 * STATE)
    keep, give = call(
        functools.partial(grad_bc_kernel, own), [(piece, F32)] * 2, [padded, (wide, F32)], smem=(0,), count=4
    )(core.reshape(1), gbc, halo, taps_bc)
    (summed,) = call(sum_kernel, [((owners * term_rows(own), LANES), F32)], count=2)(
        keep, lax.ppermute(give, "core", swap)
    )
    parts = lax.all_to_all(summed.astype(jnp.float16), ("x", "zh"), 0, 0, tiled=True).astype(F32)
    grad_x, glog = call(
        carry_kernel,
        [(wide, BF16), ((HEADS, ROWS), F32)],
        [padded, pair] + [(wide, F32)] * 3 + [((ROWS, LANES), F32)],
        hbm_in=(5, 6, 7), count=11, sems=5,
    )(*scaled, cum, features, blocks, states, both, halo, conv_x)
    (grad_bc,) = call(fold_kernel, [((own, groups * 2 * STATE), F32)], count=1)(parts)
    return grad_x, grad_bc, glog.T


def solution(mesh):
    fine = Mesh(mesh.devices.reshape(8, 2, 4, 4, 2), CTX + TP)
    return jax.shard_map(
        per_device,
        mesh=fine,
        in_specs=(P(CTX, TP), P(CTX + TP, None), P(None, TP), P(), P(CTX, TP), P(CTX, TP)),
        out_specs=(P(CTX, TP), P(CTX + TP, None), P(CTX, TP)),
        check_vma=False,
    )
```

```python
import functools

import jax
import jax.numpy as jnp
from jax import lax
from jax.experimental import pallas as pl
from jax.experimental.pallas import tpu as pltpu
from jax.sharding import Mesh, PartitionSpec as P

HEAD_DIM = 64
STATE = 256
CONV = 4
HEADS = 8
BLOCK = 256
ROWS = 512
COLS = HEADS * HEAD_DIM
BLOCKS = ROWS // BLOCK
HALO = 16
LANES = 128
META_ROWS = 8
STORE = 26

F32 = jnp.float32
BF16 = jnp.bfloat16
NN = ((1,), (0,))
NT = ((1,), (1,))
TN = ((0,), (0,))
CTX = ("y", "zl")
TP = ("x", "zh", "core")


def mul(a, b, dims):
    return lax.dot_general(a, b, (dims, ((), ())), preferred_element_type=F32)


def split2(a):
    high = a.astype(BF16)
    return high, (a - high.astype(F32)).astype(BF16)


def split3(a):
    high = a.astype(BF16)
    rest = a - high.astype(F32)
    middle = rest.astype(BF16)
    return high, middle, (rest - middle.astype(F32)).astype(BF16)


def dot3(a, b, dims):
    return mul(a[0], b[0], dims) + (mul(a[0], b[1], dims) + mul(a[1], b[0], dims))


def exact_left(ones, b, dims):
    parts = split3(b)
    return mul(ones, parts[0], dims) + (mul(ones, parts[1], dims) + mul(ones, parts[2], dims))


def exact_right(a, ones, dims):
    parts = split3(a)
    return mul(parts[0], ones, dims) + (mul(parts[1], ones, dims) + mul(parts[2], ones, dims))


def expander(rows):
    head = lax.broadcasted_iota(jnp.int32, (rows, COLS), 0)
    col = lax.broadcasted_iota(jnp.int32, (rows, COLS), 1)
    return jnp.where((col >= head * HEAD_DIM) & (col < (head + 1) * HEAD_DIM), 1.0, 0.0).astype(BF16)


def row_col(shape=(BLOCK, BLOCK)):
    return (
        lax.broadcasted_iota(jnp.int32, shape, 0),
        lax.broadcasted_iota(jnp.int32, shape, 1),
    )


def begin(sems, *pairs, first=0):
    copies = [pltpu.make_async_copy(a, b, sems.at[first + i]) for i, (a, b) in enumerate(pairs)]
    for copy in copies:
        copy.start()
    return copies


def finish(copies):
    for copy in copies:
        copy.wait()


def sigmoid(v):
    return 1.0 / (1.0 + jnp.exp(-v))


def conv(buf, prev, rows, taps):
    buf[0:8] = prev[HALO - 8 :].astype(F32)
    buf[8 : 8 + ROWS] = rows[...].astype(F32)
    pre = taps[0:1] * buf[5 : 5 + ROWS]
    for k in range(1, CONV):
        pre = pre + taps[k : k + 1] * buf[5 + k : 5 + k + ROWS]
    return pre


def group_conv(buf, prev, gathered, taps):
    cores, pairs, own, _ = gathered.shape
    buf[0:8] = prev[0][HALO - 8 :].astype(F32) + prev[1][HALO - 8 :].astype(F32)
    for pair in range(pairs):
        for core in range(cores):
            at = 8 + (pair * cores + core) * own
            buf[at : at + own] = gathered[core, pair].astype(F32)
    pre = taps[0:1] * buf[5 : 5 + ROWS]
    for k in range(1, CONV):
        pre = pre + taps[k : k + 1] * buf[5 + k : 5 + k + ROWS]
    return pre


def fan_kernel(rows_hbm, out_ref, sems):
    groups = rows_hbm.shape[1] // (2 * STATE)
    fan = out_ref.shape[0] // groups
    copies = []
    for owner in range(out_ref.shape[0]):
        at = owner // fan * (2 * STATE)
        copies += begin(sems, (rows_hbm.at[:, at : at + 2 * STATE], out_ref.at[owner]), first=owner)
    finish(copies)


def widen(values, spread):
    return exact_right(values, spread, NN)


def widen_row(row, spread):
    return widen(jnp.broadcast_to(row, (8, LANES)), spread)[0:1]


def head_sums(values, spread):
    high, low = split2(values)
    return mul(high, spread, NT) + mul(low, spread, NT)


def decay_kernel(log_ref, grad_ref, ge_hi, ge_lo, cum_ref, cumt_ref):
    row, col = row_col()
    upper = jnp.where(row <= col, 1.0, 0.0).astype(BF16)
    lower = jnp.where(col <= row, 1.0, 0.0).astype(BF16)
    spread = expander(LANES)
    before = jnp.zeros((1, LANES), F32)
    for b in range(BLOCKS):
        part = slice(b * BLOCK, (b + 1) * BLOCK)
        logs = log_ref[:, part]
        padded = jnp.concatenate([logs, jnp.zeros((LANES - HEADS, BLOCK), F32)], axis=0)
        cum = exact_left(lower, padded, NT)
        cum_ref[part] = cum
        cumt_ref[b] = exact_right(logs, upper, NN)
        ge_hi[part], ge_lo[part] = split2(grad_ref[part].astype(F32) * widen(jnp.exp(before + cum), spread))
        before = before + cum[BLOCK - 1 : BLOCK]


def feature_kernel(x_ref, prev_ref, taps_ref, cum_ref, store, xf_hi, xf_lo, buf, act_ref, slope_ref, sems):
    pre = conv(buf, prev_ref, x_ref, taps_ref)
    gate = sigmoid(pre)
    act = pre * gate
    act_ref[...] = act
    slope_ref[...] = gate * (1.0 + pre * (1.0 - gate))
    leaving = begin(sems, (act_ref, store.at[0]), (slope_ref, store.at[1]))
    xf_hi[...], xf_lo[...] = split2(act * chunk_fade(cum_ref, ROWS, expander(LANES)))
    finish(leaving)


def chunk_fade(cum_ref, rows, spread):
    parts = []
    for b in range(-(-rows // BLOCK)):
        until = -cum_ref[b * BLOCK : min((b + 1) * BLOCK, rows)]
        for later in range(b, BLOCKS):
            until = until + cum_ref[(later + 1) * BLOCK - 1 : (later + 1) * BLOCK]
        parts.append(widen(jnp.exp(until), spread))
    return parts[0] if len(parts) == 1 else jnp.concatenate(parts, axis=0)


def power_scale(values):
    top = jnp.max(jnp.max(jnp.abs(values), axis=1, keepdims=True), axis=0, keepdims=True)
    return jnp.clip(14.0 - jnp.ceil(jnp.log2(jnp.maximum(top, 1e-30))), -100.0, 100.0)


def pack_piece(first, second, out, place, logs):
    count = first.shape[0]
    ups = [power_scale(first), power_scale(second)]
    for which, array in enumerate((first, second)):
        scaled = array * jnp.exp2(ups[which])
        for t in range(COLS // LANES):
            at = (which * (COLS // LANES) + t) * count
            out[place, at : at + count] = scaled[:, t * LANES : (t + 1) * LANES]
    lane = lax.broadcasted_iota(jnp.int32, (META_ROWS, LANES), 1)
    meta = jnp.where(lane == 16, ups[0], jnp.where(lane == 17, ups[1], 0.0))
    out[place, piece_rows(count) - META_ROWS :] = jnp.where(lane < 16, logs, meta)


def piece_rows(count):
    return 2 * count * (COLS // LANES) + META_ROWS


def unpack_piece(got, place, count, which):
    meta = got[place, piece_rows(count) - META_ROWS :]
    down = jnp.exp2(-meta[0:1, 16 + which : 17 + which])
    first = which * (COLS // LANES) * count
    return [got[place, first + t * count : first + (t + 1) * count] * down for t in range(COLS // LANES)]


def state_kernel(places, bc_ref, prev_0, prev_1, taps_ref, xf_hi, xf_lo, ge_hi, ge_lo, cum_ref, pack_ref, buf):
    pre = group_conv(buf, (prev_0, prev_1), bc_ref, taps_ref)
    act = pre * sigmoid(pre)
    keys = split2(act[:, 0:STATE])
    queries = split2(act[:, STATE:])
    state = dot3(keys, (xf_hi[...], xf_lo[...]), TN)
    grad = dot3(queries, (ge_hi[...], ge_lo[...]), TN)
    total = jnp.zeros((1, LANES), F32)
    for b in range(BLOCKS):
        total = total + cum_ref[(b + 1) * BLOCK - 1 : (b + 1) * BLOCK]
    high = total.astype(BF16).astype(F32)
    lane = lax.broadcasted_iota(jnp.int32, (1, LANES), 1)
    logs = jnp.where(lane < 8, high, pltpu.roll(total - high, 8, 1))
    count = STATE // places
    for p in range(places):
        rows = slice(p * count, (p + 1) * count)
        pack_piece(state[rows], grad[rows], pack_ref, p, logs)


def term_rows(own):
    return own * (2 * STATE // LANES) + META_ROWS


def sum_kernel(keep_ref, got_ref, out_ref):
    own = keep_ref.shape[1]
    for owner in range(keep_ref.shape[0]):
        terms = keep_ref[owner] + got_ref[owner]
        up = power_scale(terms)
        scaled = terms * jnp.exp2(up)
        for t in range(2 * STATE // LANES):
            out_ref[owner, t * own : (t + 1) * own] = scaled[:, t * LANES : (t + 1) * LANES]
        out_ref[owner, term_rows(own) - META_ROWS :] = jnp.broadcast_to(up, (META_ROWS, LANES))


def fold_kernel(parts_ref, out_ref):
    own = out_ref.shape[0]
    groups = out_ref.shape[1] // (2 * STATE)
    fan = parts_ref.shape[0] // groups
    for group in range(groups):
        downs = []
        for one in range(fan):
            end = term_rows(own)
            downs.append(jnp.exp2(-parts_ref[group * fan + one, end - META_ROWS : end - META_ROWS + 1]))
        for t in range(2 * STATE // LANES):
            total = jnp.zeros((own, LANES), F32)
            for one in range(fan):
                total = total + parts_ref[group * fan + one, t * own : (t + 1) * own] * downs[one]
            at = group * 2 * STATE + t * LANES
            out_ref[:, at : at + LANES] = total


def scan_kernel(places, got_ref, out_ref):
    count = STATE // places
    spread = expander(LANES)
    lane = lax.broadcasted_iota(jnp.int32, (META_ROWS, LANES), 1)
    tiles = COLS // LANES
    decays = []
    for p in range(places):
        meta = got_ref[p, piece_rows(count) - META_ROWS :]
        logs = meta + pltpu.roll(meta, LANES - 8, 1)
        decay = jnp.where(lane < 8, jnp.exp(jnp.minimum(logs, 0.0)), 0.0)
        decays.append(widen(decay, spread)[0:1])
    coming = jnp.zeros((count, COLS), F32)
    befores = []
    for p in range(places):
        befores.append(coming)
        coming = decays[p] * coming + jnp.concatenate(unpack_piece(got_ref, p, count, 0), axis=1)
    going = jnp.zeros((count, COLS), F32)
    for p in reversed(range(places)):
        pack_piece(befores[p], going, out_ref, p, 0.0)
        going = decays[p] * going + jnp.concatenate(unpack_piece(got_ref, p, count, 1), axis=1)


def diagonal(b, act_ref, grad_ref, cum_ref, cumt_ref, bc_hi, bc_lo, dx_ref, dbc_ref, dlog_ref):
    row, col = row_col()
    causal = row <= col
    later = jnp.where(col >= row, 1.0, 0.0).astype(BF16)
    part = slice(b * BLOCK, (b + 1) * BLOCK)
    keys = (bc_hi[part, 0:STATE], bc_lo[part, 0:STATE])
    queries = (bc_hi[part, STATE:], bc_lo[part, STATE:])
    scores = dot3(keys, queries, NT)
    total = jnp.zeros((BLOCK, BLOCK), F32)
    across, down = [], []
    for h in range(HEADS):
        cols = slice(h * HEAD_DIM, (h + 1) * HEAD_DIM)
        gap = cumt_ref[b, h : h + 1, :] - cum_ref[part, h : h + 1]
        mixing = jnp.where(causal, jnp.exp(jnp.where(causal, gap, 0.0)), 0.0)
        grads = grad_ref[part, cols]
        values = split2(act_ref[part, cols])
        pairs = mixing * (mul(values[0], grads, NT) + mul(values[1], grads, NT))
        total = total + pairs
        weights = pairs * scores
        across.append(jnp.sum(weights, axis=0, keepdims=True))
        down.append(jnp.sum(weights, axis=1, keepdims=True))
        mixed = split2(mixing * scores)
        dx_ref[part, cols] = mul(mixed[0], grads, NN) + mul(mixed[1], grads, NN)
    pairs = split2(total)
    dbc_ref[part, 0:STATE] = dot3(pairs, queries, NN)
    dbc_ref[part, STATE:] = dot3(pairs, keys, TN)
    dlog_ref[part, 0:HEADS] = exact_left(later, jnp.concatenate(across, axis=0), NT) - exact_left(
        later, jnp.concatenate(down, axis=1), NN
    )


def first_kernel(features, grad_ref, bc_ref, prev_0, prev_1, taps_ref, cum_ref, cumt_ref, store,
                 act_ref, dx_ref, dbc_ref, slope_ref, bc_act, dlog_ref, bc_hi, bc_lo, buf, sems):
    coming = begin(sems, (features.at[0], act_ref))
    pre = group_conv(buf, (prev_0, prev_1), bc_ref, taps_ref)
    gate = sigmoid(pre)
    slope_ref[...] = gate * (1.0 + pre * (1.0 - gate))
    bc_act[...] = pre * gate
    leaving = begin(sems, (slope_ref, store.at[2]), (bc_act, store.at[3]), first=1)
    bc_hi[...], bc_lo[...] = split2(bc_act[...])
    finish(coming)
    diagonal(0, act_ref, grad_ref, cum_ref, cumt_ref, bc_hi, bc_lo, dx_ref, dbc_ref, dlog_ref)
    rows = slice(0, BLOCK)
    leaving += begin(
        sems, (dx_ref.at[rows], store.at[0, rows]), (dbc_ref.at[rows], store.at[1, rows]),
        (dlog_ref.at[rows], store.at[4, rows, 0:LANES]), first=3,
    )
    finish(leaving)


def second_kernel(features, early, grad_ref, cum_ref, cumt_ref, store,
                  act_ref, dx_ref, dbc_ref, bc_act, dlog_ref, bc_hi, bc_lo, sems):
    rows = slice(0, BLOCK)
    coming = begin(
        sems, (features.at[0], act_ref), (early.at[3], bc_act), (early.at[0, rows], dx_ref.at[rows]),
        (early.at[1, rows], dbc_ref.at[rows]), (early.at[4, rows, 0:LANES], dlog_ref.at[rows]),
    )
    leaving = begin(sems, (early.at[2], store.at[2]), (early.at[3], store.at[3]), first=5)
    finish(coming)
    bc_hi[...], bc_lo[...] = split2(bc_act[...])
    diagonal(1, act_ref, grad_ref, cum_ref, cumt_ref, bc_hi, bc_lo, dx_ref, dbc_ref, dlog_ref)
    row, col = row_col()
    later = jnp.where(col >= row, 1.0, 0.0).astype(BF16)
    before = jnp.where(col < row, 1.0, 0.0).astype(BF16)
    spread = expander(LANES)
    first, second = slice(0, BLOCK), slice(BLOCK, 2 * BLOCK)
    last = cum_ref[BLOCK - 1 : BLOCK]
    fade = widen(jnp.exp(last - cum_ref[first]), spread)
    faded = act_ref[first] * fade
    grown = grad_ref[second].astype(F32) * widen(jnp.exp(cum_ref[second]), spread)
    faded2, grown2 = split2(faded), split2(grown)
    keys = (bc_hi[first, 0:STATE], bc_lo[first, 0:STATE])
    queries = (bc_hi[second, STATE:], bc_lo[second, STATE:])
    scores = split2(dot3(keys, queries, NT))
    pairs = split2(dot3(faded2, grown2, NT))
    dbc_ref[first, 0:STATE] += dot3(pairs, queries, NN)
    dbc_ref[second, STATE:] += dot3(pairs, keys, TN)
    pulls = dot3(scores, grown2, NN)
    reads = dot3(scores, faded2, TN)
    dx_ref[first] += fade * pulls
    dlog_ref[first, 0:HEADS] += exact_left(before, head_sums(faded * pulls, spread), NN)[:, 0:HEADS]
    dlog_ref[second, 0:HEADS] += exact_left(later, head_sums(grown * reads, spread), NN)[:, 0:HEADS]
    leaving += begin(
        sems, (dx_ref, store.at[0]), (dbc_ref, store.at[1]), (dlog_ref, store.at[4, :, 0:LANES]), first=7
    )
    finish(leaving)


def unpack_states(places, got_ref, which, out):
    count = STATE // places
    for p in range(places):
        for t, tile in enumerate(unpack_piece(got_ref, p, count, which)):
            out[p * count : (p + 1) * count, t * LANES : (t + 1) * LANES] = tile


def open_kernel(places, got_ref, xf_hi, xf_lo, ge_hi, ge_lo, cum_ref, features, blocks,
                store, both_ref, halo_ref, coming, going, states, dx, dbc, slope, bc_act, xslope, sems):
    top = slice(0, HALO)
    arriving = begin(
        sems, (blocks.at[0, top], dx), (blocks.at[1, top], dbc), (blocks.at[2, top], slope),
        (blocks.at[3, top], bc_act), (features.at[1, top], xslope),
    )
    unpack_states(places, got_ref, 0, coming)
    unpack_states(places, got_ref, 1, going)
    enter = split2(coming[...])
    leave = split2(going[...])
    states[0, 0:STATE], states[0, STATE:] = enter
    states[1, 0:STATE], states[1, STATE:] = leave
    leaving = begin(sems, (states, store.at[0:2]), first=5)
    both_ref[...] = jnp.broadcast_to(jnp.sum(coming[...] * going[...], axis=0, keepdims=True), (8, COLS))
    fade = chunk_fade(cum_ref, HALO, expander(LANES))
    finish(arriving)
    pulls = dot3(split2(bc_act[:, 0:STATE]), leave, NN)
    keys = dbc[:, 0:STATE] + dot3((xf_hi[top], xf_lo[top]), leave, NT)
    queries = dbc[:, STATE:] + dot3((ge_hi[top], ge_lo[top]), enter, NT)
    gx = (dx[...] + fade * pulls) * xslope[...]
    halo_ref[:, 0:COLS] = gx[0:8]
    halo_ref[:, COLS : COLS + STATE] = (keys * slope[:, 0:STATE])[0:8]
    halo_ref[:, COLS + STATE :] = (queries * slope[:, STATE:])[0:8]
    finish(leaving)


def group_kernel(xf_hi, xf_lo, ge_hi, ge_lo, blocks, store, gbc_ref, states, dbc_ref, slope_ref, sems):
    first = begin(sems, (store.at[0:2], states))
    arriving = begin(sems, (blocks.at[1], dbc_ref), (blocks.at[2], slope_ref), first=1)
    finish(first)
    keys = dot3((xf_hi[...], xf_lo[...]), (states[1, 0:STATE], states[1, STATE:]), NT)
    queries = dot3((ge_hi[...], ge_lo[...]), (states[0, 0:STATE], states[0, STATE:]), NT)
    finish(arriving)
    gbc_ref[:, 0:STATE] = (dbc_ref[:, 0:STATE] + keys) * slope_ref[:, 0:STATE]
    gbc_ref[:, STATE:] = (dbc_ref[:, STATE:] + queries) * slope_ref[:, STATE:]


def back_conv(buf, taps):
    out = taps[0:1] * buf[3 : 3 + ROWS]
    for k in range(1, CONV):
        out = out + taps[k : k + 1] * buf[3 - k : 3 - k + ROWS]
    return out


def grad_bc_kernel(own, core_ref, rows_ref, halo_ref, taps_ref, keep_ref, give_ref, buf, terms):
    buf[0:ROWS] = rows_ref[...]
    buf[ROWS : ROWS + 8] = halo_ref[:, COLS:]
    terms[...] = back_conv(buf, taps_ref)
    core = core_ref[0]
    for pair in range(ROWS // (2 * own)):
        at = pair * 2 * own
        keep_ref[pair] = terms[pl.ds(pl.multiple_of(at + core * own, own), own)]
        give_ref[pair] = terms[pl.ds(pl.multiple_of(at + (1 - core) * own, own), own)]


def carry_kernel(xf_hi, xf_lo, ge_hi, ge_lo, cum_ref, features, blocks, store, both_ref, halo_ref, taps_ref,
                 grad_ref, glog_ref, buf, states, bc_act, dx_ref, xslope_ref, dlog_ref, sems):
    arriving = begin(
        sems, (store.at[0:2], states), (blocks.at[3], bc_act), (blocks.at[0], dx_ref),
        (features.at[1], xslope_ref), (blocks.at[4, :, 0:LANES], dlog_ref),
    )
    spread = expander(LANES)
    fade = chunk_fade(cum_ref, ROWS, spread)
    finish(arriving)
    pulls = dot3(split2(bc_act[:, 0:STATE]), (states[1, 0:STATE], states[1, STATE:]), NN)
    buf[0:ROWS] = (dx_ref[...] + fade * pulls) * xslope_ref[...]
    buf[ROWS : ROWS + 8] = halo_ref[:, 0:COLS]
    grad_ref[...] = back_conv(buf, taps_ref).astype(BF16)
    reads = dot3(split2(bc_act[:, STATE:]), (states[0, 0:STATE], states[0, STATE:]), NN)
    grown = ge_hi[...].astype(F32) + ge_lo[...].astype(F32)
    faded = xf_hi[...].astype(F32) + xf_lo[...].astype(F32)
    across = head_sums(grown * reads, spread)
    down = head_sums(faded * pulls, spread)
    last = jnp.zeros((1, LANES), F32)
    for b in range(BLOCKS):
        last = last + cum_ref[(b + 1) * BLOCK - 1 : (b + 1) * BLOCK]
    both = head_sums(both_ref[...], spread)[0:1] * jnp.exp(last)
    row, col = row_col((ROWS, ROWS))
    later = jnp.where(col >= row, 1.0, 0.0).astype(BF16)
    before = jnp.where(col < row, 1.0, 0.0).astype(BF16)
    found = dlog_ref[...] + exact_left(later, across, NN) + exact_left(before, down, NN) + both
    glog_ref[...] = jnp.transpose(found)[0:HEADS]


def call(kernel, outs, scratch=(), hbm_in=(), hbm_out=(), smem=(), fused=(), count=0, sems=0, vmem=40, flops=1 << 26, size=1 << 22):
    def place(i, far):
        return pl.BlockSpec(memory_space=pltpu.SMEM if i in smem else pltpu.HBM if i in far else pltpu.VMEM)

    return pl.pallas_call(
        kernel,
        out_shape=[jax.ShapeDtypeStruct(shape, dtype) for shape, dtype in outs],
        in_specs=[place(i, hbm_in) for i in range(count)],
        out_specs=[
            pl.BlockSpec(memory_space=pltpu.HBM if i in hbm_out else pltpu.VMEM) for i in range(len(outs))
        ],
        scratch_shapes=[pltpu.VMEM(shape, dtype) for shape, dtype in scratch]
        + ([pltpu.SemaphoreType.DMA((sems,))] if sems else []),
        compiler_params=pltpu.CompilerParams(
            vmem_limit_bytes=vmem * 2**20,
            allow_input_fusion=[i in fused for i in range(count)] if fused else None,
        ),
        cost_estimate=pl.CostEstimate(flops=flops, bytes_accessed=size, transcendentals=0),
    )


def shifted(array, by):
    devices = lax.axis_size(CTX)
    pairs = [(i, i + by) for i in range(devices) if 0 <= i + by < devices]
    return lax.ppermute(array, CTX, pairs)


def per_device(x_in, bc_in, conv_x, conv_bc, log_decay, grad_y):
    core = lax.axis_index("core")
    owners = lax.axis_size(("x", "zh"))
    places = lax.axis_size(CTX)
    groups = bc_in.shape[1] // (2 * STATE)
    own = bc_in.shape[0]
    fan = owners // groups
    group = lax.axis_index(("x", "zh")) // fan
    taps_bc = lax.dynamic_slice_in_dim(conv_bc, group * (2 * STATE), 2 * STATE, 1)
    swap = [(0, 1), (1, 0)]

    (spread,) = call(
        fan_kernel, [((owners, own, 2 * STATE), BF16)], hbm_in=(0,), count=1, sems=owners, vmem=62
    )(bc_in)
    mine = lax.all_to_all(spread, ("x", "zh"), 0, 0, tiled=True)
    x_prev = shifted(x_in[ROWS - HALO :], 1)
    wide = (ROWS, COLS)
    padded = ((ROWS + 8, COLS), F32)
    store = (STORE,) + wide
    ge_hi, ge_lo, cum, cumt = call(
        decay_kernel, [(wide, BF16)] * 2 + [((ROWS, LANES), F32), ((BLOCKS, HEADS, BLOCK), F32)], count=2
    )(log_decay.T, grad_y)
    made = call(
        feature_kernel, [(store, F32)] + [(wide, BF16)] * 2, [padded, (wide, F32), (wide, F32)],
        hbm_out=(0,), count=4, sems=2,
    )(x_in, x_prev, conv_x, cum)
    mine, made = lax.optimization_barrier((mine, made))
    features, xf_hi, xf_lo = made
    scaled = (xf_hi, xf_lo, ge_hi, ge_lo)
    bc_prev = [
        lax.ppermute(
            mine[owners - 1], CTX + ("core",), [(2 * i + 1, 2 * (i + 1) + to) for i in range(places - 1)]
        )
        for to in (0, 1)
    ]
    bc_rows = lax.all_gather(mine, "core")
    packed = (places, piece_rows(STATE // places), LANES)
    (sent,) = call(functools.partial(state_kernel, places), [(packed, F32)], [padded], count=9)(
        bc_rows, *bc_prev, taps_bc, *scaled, cum
    )
    got = lax.all_to_all(sent.astype(jnp.float16), CTX, 0, 0, tiled=True)
    (early,) = call(
        first_kernel, [(store, F32)],
        [(wide, F32)] * 5 + [((ROWS, LANES), F32)] + [(wide, BF16)] * 2 + [padded],
        hbm_in=(0,), hbm_out=(0,), count=8, sems=6, flops=1 << 32,
    )(features, grad_y, bc_rows, *bc_prev, taps_bc, cum, cumt)
    got, early = lax.optimization_barrier((got, early))
    (back,) = call(functools.partial(scan_kernel, places), [(packed, F32)], fused=(0,), count=1)(got.astype(F32))
    early, back = lax.optimization_barrier((early, back))
    (blocks,) = call(
        second_kernel, [(store, F32)],
        [(wide, F32)] * 4 + [((ROWS, LANES), F32)] + [(wide, BF16)] * 2,
        hbm_in=(0, 1), hbm_out=(0,), count=5, sems=10, flops=1 << 32,
    )(features, early, grad_y, cum, cumt)
    carried = lax.all_to_all(back.astype(jnp.float16), CTX, 0, 0, tiled=True).astype(F32)

    half = (STATE, COLS)
    top = (HALO, COLS)
    pair = ((2,) + wide, BF16)
    states, both, first = call(
        functools.partial(open_kernel, places),
        [((2 * STORE,) + wide, BF16), ((8, COLS), F32), ((8, COLS + 2 * STATE), F32)],
        [(half, F32)] * 2 + [pair] + [(top, F32)] * 5,
        hbm_in=(6, 7), hbm_out=(0,), fused=(0,), count=8, sems=6,
    )(carried, *scaled, cum, features, blocks)
    halo = shifted(first, -1)
    (gbc,) = call(
        group_kernel, [(wide, F32)], [pair] + [(wide, F32)] * 2, hbm_in=(4, 5), count=6, sems=3
    )(*scaled, blocks, states)
    piece = (owners, own, 2 * STATE)
    keep, give = call(
        functools.partial(grad_bc_kernel, own), [(piece, F32)] * 2, [padded, (wide, F32)], smem=(0,), count=4
    )(core.reshape(1), gbc, halo, taps_bc)
    (summed,) = call(sum_kernel, [((owners, term_rows(own), LANES), F32)], count=2)(
        keep, lax.ppermute(give, "core", swap)
    )
    parts = lax.all_to_all(summed.astype(jnp.float16), ("x", "zh"), 0, 0, tiled=True).astype(F32)
    grad_x, glog = call(
        carry_kernel,
        [(wide, BF16), ((HEADS, ROWS), F32)],
        [padded, pair] + [(wide, F32)] * 3 + [((ROWS, LANES), F32)],
        hbm_in=(5, 6, 7), count=11, sems=5,
    )(*scaled, cum, features, blocks, states, both, halo, conv_x)
    (grad_bc,) = call(fold_kernel, [((own, groups * 2 * STATE), F32)], fused=(0,), count=1)(parts)
    return grad_x, grad_bc, glog.T


def solution(mesh):
    fine = Mesh(mesh.devices.reshape(8, 2, 4, 4, 2), CTX + TP)
    return jax.shard_map(
        per_device,
        mesh=fine,
        in_specs=(P(CTX, TP), P(CTX + TP, None), P(None, TP), P(), P(CTX, TP), P(CTX, TP)),
        out_specs=(P(CTX, TP), P(CTX + TP, None), P(CTX, TP)),
        check_vma=False,
    )
```

```python
import functools

import jax
import jax.numpy as jnp
from jax import lax
from jax.experimental import pallas as pl
from jax.experimental.pallas import tpu as pltpu
from jax.sharding import Mesh, PartitionSpec as P

HEAD_DIM = 64
STATE = 256
CONV = 4
HEADS = 8
BLOCK = 256
ROWS = 512
COLS = HEADS * HEAD_DIM
BLOCKS = ROWS // BLOCK
HALO = 16
LANES = 128
META_ROWS = 8
STORE = 26

F32 = jnp.float32
BF16 = jnp.bfloat16
NN = ((1,), (0,))
NT = ((1,), (1,))
TN = ((0,), (0,))
CTX = ("y", "zl")
TP = ("x", "zh", "core")


def mul(a, b, dims):
    return lax.dot_general(a, b, (dims, ((), ())), preferred_element_type=F32)


def split2(a):
    high = a.astype(BF16)
    return high, (a - high.astype(F32)).astype(BF16)


def split3(a):
    high = a.astype(BF16)
    rest = a - high.astype(F32)
    middle = rest.astype(BF16)
    return high, middle, (rest - middle.astype(F32)).astype(BF16)


def dot3(a, b, dims):
    return mul(a[0], b[0], dims) + (mul(a[0], b[1], dims) + mul(a[1], b[0], dims))


def exact_left(ones, b, dims):
    parts = split3(b)
    return mul(ones, parts[0], dims) + (mul(ones, parts[1], dims) + mul(ones, parts[2], dims))


def exact_right(a, ones, dims):
    parts = split3(a)
    return mul(parts[0], ones, dims) + (mul(parts[1], ones, dims) + mul(parts[2], ones, dims))


def expander(rows):
    head = lax.broadcasted_iota(jnp.int32, (rows, COLS), 0)
    col = lax.broadcasted_iota(jnp.int32, (rows, COLS), 1)
    return jnp.where((col >= head * HEAD_DIM) & (col < (head + 1) * HEAD_DIM), 1.0, 0.0).astype(BF16)


def row_col(shape=(BLOCK, BLOCK)):
    return (
        lax.broadcasted_iota(jnp.int32, shape, 0),
        lax.broadcasted_iota(jnp.int32, shape, 1),
    )


def begin(sems, *pairs, first=0):
    copies = [pltpu.make_async_copy(a, b, sems.at[first + i]) for i, (a, b) in enumerate(pairs)]
    for copy in copies:
        copy.start()
    return copies


def finish(copies):
    for copy in copies:
        copy.wait()


def sigmoid(v):
    return 1.0 / (1.0 + jnp.exp(-v))


def conv(buf, prev, rows, taps):
    buf[0:8] = prev[HALO - 8 :].astype(F32)
    buf[8 : 8 + ROWS] = rows[...].astype(F32)
    pre = taps[0:1] * buf[5 : 5 + ROWS]
    for k in range(1, CONV):
        pre = pre + taps[k : k + 1] * buf[5 + k : 5 + k + ROWS]
    return pre


def group_conv(buf, prev, gathered, taps):
    cores, pairs, own, _ = gathered.shape
    buf[0:8] = prev[0][HALO - 8 :].astype(F32) + prev[1][HALO - 8 :].astype(F32)
    for pair in range(pairs):
        for core in range(cores):
            at = 8 + (pair * cores + core) * own
            buf[at : at + own] = gathered[core, pair].astype(F32)
    pre = taps[0:1] * buf[5 : 5 + ROWS]
    for k in range(1, CONV):
        pre = pre + taps[k : k + 1] * buf[5 + k : 5 + k + ROWS]
    return pre


def fan_kernel(rows_hbm, out_ref, sems):
    groups = rows_hbm.shape[1] // (2 * STATE)
    fan = out_ref.shape[0] // groups
    copies = []
    for owner in range(out_ref.shape[0]):
        at = owner // fan * (2 * STATE)
        copies += begin(sems, (rows_hbm.at[:, at : at + 2 * STATE], out_ref.at[owner]), first=owner)
    finish(copies)


def widen(values, spread):
    return exact_right(values, spread, NN)


def widen_row(row, spread):
    return widen(jnp.broadcast_to(row, (8, LANES)), spread)[0:1]


def head_sums(values, spread):
    high, low = split2(values)
    return mul(high, spread, NT) + mul(low, spread, NT)


def decay_kernel(log_ref, grad_ref, ge_hi, ge_lo, cum_ref, cumt_ref):
    row, col = row_col()
    upper = jnp.where(row <= col, 1.0, 0.0).astype(BF16)
    lower = jnp.where(col <= row, 1.0, 0.0).astype(BF16)
    spread = expander(LANES)
    before = jnp.zeros((1, LANES), F32)
    for b in range(BLOCKS):
        part = slice(b * BLOCK, (b + 1) * BLOCK)
        logs = log_ref[:, part]
        padded = jnp.concatenate([logs, jnp.zeros((LANES - HEADS, BLOCK), F32)], axis=0)
        cum = exact_left(lower, padded, NT)
        cum_ref[part] = cum
        cumt_ref[b] = exact_right(logs, upper, NN)
        ge_hi[part], ge_lo[part] = split2(grad_ref[part].astype(F32) * widen(jnp.exp(before + cum), spread))
        before = before + cum[BLOCK - 1 : BLOCK]


def feature_kernel(x_ref, prev_ref, taps_ref, cum_ref, store, xf_hi, xf_lo, buf, act_ref, slope_ref, sems):
    pre = conv(buf, prev_ref, x_ref, taps_ref)
    gate = sigmoid(pre)
    act = pre * gate
    act_ref[...] = act
    slope_ref[...] = gate * (1.0 + pre * (1.0 - gate))
    leaving = begin(sems, (act_ref, store.at[0]), (slope_ref, store.at[1]))
    xf_hi[...], xf_lo[...] = split2(act * chunk_fade(cum_ref, ROWS, expander(LANES)))
    finish(leaving)


def chunk_fade(cum_ref, rows, spread):
    parts = []
    for b in range(-(-rows // BLOCK)):
        until = -cum_ref[b * BLOCK : min((b + 1) * BLOCK, rows)]
        for later in range(b, BLOCKS):
            until = until + cum_ref[(later + 1) * BLOCK - 1 : (later + 1) * BLOCK]
        parts.append(widen(jnp.exp(until), spread))
    return parts[0] if len(parts) == 1 else jnp.concatenate(parts, axis=0)


def power_scale(values):
    top = jnp.max(jnp.max(jnp.abs(values), axis=1, keepdims=True), axis=0, keepdims=True)
    return jnp.clip(14.0 - jnp.ceil(jnp.log2(jnp.maximum(top, 1e-30))), -100.0, 100.0)


def pack_piece(first, second, out, place, logs):
    count = first.shape[0]
    ups = [power_scale(first), power_scale(second)]
    for which, array in enumerate((first, second)):
        scaled = array * jnp.exp2(ups[which])
        for t in range(COLS // LANES):
            at = (which * (COLS // LANES) + t) * count
            out[place, at : at + count] = scaled[:, t * LANES : (t + 1) * LANES]
    lane = lax.broadcasted_iota(jnp.int32, (META_ROWS, LANES), 1)
    meta = jnp.where(lane == 16, ups[0], jnp.where(lane == 17, ups[1], 0.0))
    out[place, piece_rows(count) - META_ROWS :] = jnp.where(lane < 16, logs, meta)


def piece_rows(count):
    return 2 * count * (COLS // LANES) + META_ROWS


def unpack_piece(got, place, count, which):
    meta = got[place, piece_rows(count) - META_ROWS :]
    down = jnp.exp2(-meta[0:1, 16 + which : 17 + which])
    first = which * (COLS // LANES) * count
    return [got[place, first + t * count : first + (t + 1) * count] * down for t in range(COLS // LANES)]


def state_kernel(places, bc_ref, prev_0, prev_1, taps_ref, xf_hi, xf_lo, ge_hi, ge_lo, cum_ref, pack_ref, buf):
    pre = group_conv(buf, (prev_0, prev_1), bc_ref, taps_ref)
    act = pre * sigmoid(pre)
    keys = split2(act[:, 0:STATE])
    queries = split2(act[:, STATE:])
    state = dot3(keys, (xf_hi[...], xf_lo[...]), TN)
    grad = dot3(queries, (ge_hi[...], ge_lo[...]), TN)
    total = jnp.zeros((1, LANES), F32)
    for b in range(BLOCKS):
        total = total + cum_ref[(b + 1) * BLOCK - 1 : (b + 1) * BLOCK]
    high = total.astype(BF16).astype(F32)
    lane = lax.broadcasted_iota(jnp.int32, (1, LANES), 1)
    logs = jnp.where(lane < 8, high, pltpu.roll(total - high, 8, 1))
    count = STATE // places
    for p in range(places):
        rows = slice(p * count, (p + 1) * count)
        pack_piece(state[rows], grad[rows], pack_ref, p, logs)


def term_rows(own):
    return own * (2 * STATE // LANES) + META_ROWS


def sum_kernel(keep_ref, got_ref, out_ref):
    own = keep_ref.shape[1]
    for owner in range(keep_ref.shape[0]):
        terms = keep_ref[owner] + got_ref[owner]
        up = power_scale(terms)
        scaled = terms * jnp.exp2(up)
        for t in range(2 * STATE // LANES):
            out_ref[owner, t * own : (t + 1) * own] = scaled[:, t * LANES : (t + 1) * LANES]
        out_ref[owner, term_rows(own) - META_ROWS :] = jnp.broadcast_to(up, (META_ROWS, LANES))


def fold_kernel(parts_ref, out_ref):
    own = out_ref.shape[0]
    groups = out_ref.shape[1] // (2 * STATE)
    fan = parts_ref.shape[0] // groups
    for group in range(groups):
        downs = []
        for one in range(fan):
            end = term_rows(own)
            downs.append(jnp.exp2(-parts_ref[group * fan + one, end - META_ROWS : end - META_ROWS + 1]))
        for t in range(2 * STATE // LANES):
            total = jnp.zeros((own, LANES), F32)
            for one in range(fan):
                total = total + parts_ref[group * fan + one, t * own : (t + 1) * own] * downs[one]
            at = group * 2 * STATE + t * LANES
            out_ref[:, at : at + LANES] = total


def scan_kernel(places, got_ref, out_ref):
    count = STATE // places
    spread = expander(LANES)
    lane = lax.broadcasted_iota(jnp.int32, (META_ROWS, LANES), 1)
    tiles = COLS // LANES
    decays = []
    for p in range(places):
        meta = got_ref[p, piece_rows(count) - META_ROWS :]
        logs = meta + pltpu.roll(meta, LANES - 8, 1)
        decay = jnp.where(lane < 8, jnp.exp(jnp.minimum(logs, 0.0)), 0.0)
        decays.append(widen(decay, spread)[0:1])
    coming = jnp.zeros((count, COLS), F32)
    befores = []
    for p in range(places):
        befores.append(coming)
        coming = decays[p] * coming + jnp.concatenate(unpack_piece(got_ref, p, count, 0), axis=1)
    going = jnp.zeros((count, COLS), F32)
    for p in reversed(range(places)):
        pack_piece(befores[p], going, out_ref, p, 0.0)
        going = decays[p] * going + jnp.concatenate(unpack_piece(got_ref, p, count, 1), axis=1)


def diagonal(b, act_ref, grad_ref, cum_ref, cumt_ref, bc_hi, bc_lo, dx_ref, dbc_ref, dlog_ref):
    row, col = row_col()
    causal = row <= col
    later = jnp.where(col >= row, 1.0, 0.0).astype(BF16)
    part = slice(b * BLOCK, (b + 1) * BLOCK)
    keys = (bc_hi[part, 0:STATE], bc_lo[part, 0:STATE])
    queries = (bc_hi[part, STATE:], bc_lo[part, STATE:])
    scores = dot3(keys, queries, NT)
    total = jnp.zeros((BLOCK, BLOCK), F32)
    across, down = [], []
    for h in range(HEADS):
        cols = slice(h * HEAD_DIM, (h + 1) * HEAD_DIM)
        gap = cumt_ref[b, h : h + 1, :] - cum_ref[part, h : h + 1]
        mixing = jnp.where(causal, jnp.exp(jnp.where(causal, gap, 0.0)), 0.0)
        grads = grad_ref[part, cols]
        values = split2(act_ref[part, cols])
        pairs = mixing * (mul(values[0], grads, NT) + mul(values[1], grads, NT))
        total = total + pairs
        weights = pairs * scores
        across.append(jnp.sum(weights, axis=0, keepdims=True))
        down.append(jnp.sum(weights, axis=1, keepdims=True))
        mixed = split2(mixing * scores)
        dx_ref[part, cols] = mul(mixed[0], grads, NN) + mul(mixed[1], grads, NN)
    pairs = split2(total)
    dbc_ref[part, 0:STATE] = dot3(pairs, queries, NN)
    dbc_ref[part, STATE:] = dot3(pairs, keys, TN)
    dlog_ref[part, 0:HEADS] = exact_left(later, jnp.concatenate(across, axis=0), NT) - exact_left(
        later, jnp.concatenate(down, axis=1), NN
    )


def first_kernel(features, grad_ref, bc_ref, prev_0, prev_1, taps_ref, cum_ref, cumt_ref, store,
                 act_ref, dx_ref, dbc_ref, slope_ref, bc_act, dlog_ref, bc_hi, bc_lo, buf, sems):
    coming = begin(sems, (features.at[0], act_ref))
    pre = group_conv(buf, (prev_0, prev_1), bc_ref, taps_ref)
    gate = sigmoid(pre)
    slope_ref[...] = gate * (1.0 + pre * (1.0 - gate))
    bc_act[...] = pre * gate
    leaving = begin(sems, (slope_ref, store.at[2]), (bc_act, store.at[3]), first=1)
    bc_hi[...], bc_lo[...] = split2(bc_act[...])
    finish(coming)
    diagonal(0, act_ref, grad_ref, cum_ref, cumt_ref, bc_hi, bc_lo, dx_ref, dbc_ref, dlog_ref)
    rows = slice(0, BLOCK)
    leaving += begin(
        sems, (dx_ref.at[rows], store.at[0, rows]), (dbc_ref.at[rows], store.at[1, rows]),
        (dlog_ref.at[rows], store.at[4, rows, 0:LANES]), first=3,
    )
    finish(leaving)


def second_kernel(features, early, grad_ref, cum_ref, cumt_ref, store,
                  act_ref, dx_ref, dbc_ref, slope_ref, bc_act, dlog_ref, bc_hi, bc_lo, sems):
    rows = slice(0, BLOCK)
    coming = begin(
        sems, (features.at[0], act_ref), (early.at[3], bc_act), (early.at[0, rows], dx_ref.at[rows]),
        (early.at[1, rows], dbc_ref.at[rows]), (early.at[4, rows, 0:LANES], dlog_ref.at[rows]),
        (early.at[2], slope_ref),
    )
    finish(coming)
    leaving = begin(sems, (slope_ref, store.at[2]), (bc_act, store.at[3]), first=6)
    bc_hi[...], bc_lo[...] = split2(bc_act[...])
    diagonal(1, act_ref, grad_ref, cum_ref, cumt_ref, bc_hi, bc_lo, dx_ref, dbc_ref, dlog_ref)
    row, col = row_col()
    later = jnp.where(col >= row, 1.0, 0.0).astype(BF16)
    before = jnp.where(col < row, 1.0, 0.0).astype(BF16)
    spread = expander(LANES)
    first, second = slice(0, BLOCK), slice(BLOCK, 2 * BLOCK)
    last = cum_ref[BLOCK - 1 : BLOCK]
    fade = widen(jnp.exp(last - cum_ref[first]), spread)
    faded = act_ref[first] * fade
    grown = grad_ref[second].astype(F32) * widen(jnp.exp(cum_ref[second]), spread)
    faded2, grown2 = split2(faded), split2(grown)
    keys = (bc_hi[first, 0:STATE], bc_lo[first, 0:STATE])
    queries = (bc_hi[second, STATE:], bc_lo[second, STATE:])
    scores = split2(dot3(keys, queries, NT))
    pairs = split2(dot3(faded2, grown2, NT))
    dbc_ref[first, 0:STATE] += dot3(pairs, queries, NN)
    dbc_ref[second, STATE:] += dot3(pairs, keys, TN)
    pulls = dot3(scores, grown2, NN)
    reads = dot3(scores, faded2, TN)
    dx_ref[first] += fade * pulls
    dlog_ref[first, 0:HEADS] += exact_left(before, head_sums(faded * pulls, spread), NN)[:, 0:HEADS]
    dlog_ref[second, 0:HEADS] += exact_left(later, head_sums(grown * reads, spread), NN)[:, 0:HEADS]
    leaving += begin(
        sems, (dx_ref, store.at[0]), (dbc_ref, store.at[1]), (dlog_ref, store.at[4, :, 0:LANES]), first=8
    )
    finish(leaving)


def unpack_states(places, got_ref, which, out):
    count = STATE // places
    for p in range(places):
        for t, tile in enumerate(unpack_piece(got_ref, p, count, which)):
            out[p * count : (p + 1) * count, t * LANES : (t + 1) * LANES] = tile


def open_kernel(places, got_ref, xf_hi, xf_lo, ge_hi, ge_lo, cum_ref, features, blocks,
                store, both_ref, halo_ref, coming, going, states, dx, dbc, slope, bc_act, xslope, sems):
    top = slice(0, HALO)
    arriving = begin(
        sems, (blocks.at[0, top], dx), (blocks.at[1, top], dbc), (blocks.at[2, top], slope),
        (blocks.at[3, top], bc_act), (features.at[1, top], xslope),
    )
    unpack_states(places, got_ref, 0, coming)
    unpack_states(places, got_ref, 1, going)
    enter = split2(coming[...])
    leave = split2(going[...])
    states[0, 0:STATE], states[0, STATE:] = enter
    states[1, 0:STATE], states[1, STATE:] = leave
    leaving = begin(sems, (states, store.at[0:2]), first=5)
    both_ref[...] = jnp.broadcast_to(jnp.sum(coming[...] * going[...], axis=0, keepdims=True), (8, COLS))
    fade = chunk_fade(cum_ref, HALO, expander(LANES))
    finish(arriving)
    pulls = dot3(split2(bc_act[:, 0:STATE]), leave, NN)
    keys = dbc[:, 0:STATE] + dot3((xf_hi[top], xf_lo[top]), leave, NT)
    queries = dbc[:, STATE:] + dot3((ge_hi[top], ge_lo[top]), enter, NT)
    gx = (dx[...] + fade * pulls) * xslope[...]
    halo_ref[:, 0:COLS] = gx[0:8]
    halo_ref[:, COLS : COLS + STATE] = (keys * slope[:, 0:STATE])[0:8]
    halo_ref[:, COLS + STATE :] = (queries * slope[:, STATE:])[0:8]
    finish(leaving)


def group_kernel(xf_hi, xf_lo, ge_hi, ge_lo, blocks, store, gbc_ref, states, dbc_ref, slope_ref, sems):
    first = begin(sems, (store.at[0:2], states))
    arriving = begin(sems, (blocks.at[1], dbc_ref), (blocks.at[2], slope_ref), first=1)
    finish(first)
    keys = dot3((xf_hi[...], xf_lo[...]), (states[1, 0:STATE], states[1, STATE:]), NT)
    queries = dot3((ge_hi[...], ge_lo[...]), (states[0, 0:STATE], states[0, STATE:]), NT)
    finish(arriving)
    gbc_ref[:, 0:STATE] = (dbc_ref[:, 0:STATE] + keys) * slope_ref[:, 0:STATE]
    gbc_ref[:, STATE:] = (dbc_ref[:, STATE:] + queries) * slope_ref[:, STATE:]


def back_conv(buf, taps):
    out = taps[0:1] * buf[3 : 3 + ROWS]
    for k in range(1, CONV):
        out = out + taps[k : k + 1] * buf[3 - k : 3 - k + ROWS]
    return out


def grad_bc_kernel(own, core_ref, rows_ref, halo_ref, taps_ref, keep_ref, give_ref, buf, terms):
    buf[0:ROWS] = rows_ref[...]
    buf[ROWS : ROWS + 8] = halo_ref[:, COLS:]
    terms[...] = back_conv(buf, taps_ref)
    core = core_ref[0]
    for pair in range(ROWS // (2 * own)):
        at = pair * 2 * own
        keep_ref[pair] = terms[pl.ds(pl.multiple_of(at + core * own, own), own)]
        give_ref[pair] = terms[pl.ds(pl.multiple_of(at + (1 - core) * own, own), own)]


def carry_kernel(xf_hi, xf_lo, ge_hi, ge_lo, cum_ref, features, blocks, store, both_ref, halo_ref, taps_ref,
                 grad_ref, glog_ref, buf, states, bc_act, dx_ref, xslope_ref, dlog_ref, sems):
    arriving = begin(
        sems, (store.at[0:2], states), (blocks.at[3], bc_act), (blocks.at[0], dx_ref),
        (features.at[1], xslope_ref), (blocks.at[4, :, 0:LANES], dlog_ref),
    )
    spread = expander(LANES)
    fade = chunk_fade(cum_ref, ROWS, spread)
    finish(arriving)
    pulls = dot3(split2(bc_act[:, 0:STATE]), (states[1, 0:STATE], states[1, STATE:]), NN)
    buf[0:ROWS] = (dx_ref[...] + fade * pulls) * xslope_ref[...]
    buf[ROWS : ROWS + 8] = halo_ref[:, 0:COLS]
    grad_ref[...] = back_conv(buf, taps_ref).astype(BF16)
    reads = dot3(split2(bc_act[:, STATE:]), (states[0, 0:STATE], states[0, STATE:]), NN)
    grown = ge_hi[...].astype(F32) + ge_lo[...].astype(F32)
    faded = xf_hi[...].astype(F32) + xf_lo[...].astype(F32)
    across = head_sums(grown * reads, spread)
    down = head_sums(faded * pulls, spread)
    last = jnp.zeros((1, LANES), F32)
    for b in range(BLOCKS):
        last = last + cum_ref[(b + 1) * BLOCK - 1 : (b + 1) * BLOCK]
    both = head_sums(both_ref[...], spread)[0:1] * jnp.exp(last)
    row, col = row_col((ROWS, ROWS))
    later = jnp.where(col >= row, 1.0, 0.0).astype(BF16)
    before = jnp.where(col < row, 1.0, 0.0).astype(BF16)
    found = dlog_ref[...] + exact_left(later, across, NN) + exact_left(before, down, NN) + both
    glog_ref[...] = jnp.transpose(found)[0:HEADS]


def call(kernel, outs, scratch=(), hbm_in=(), hbm_out=(), smem=(), fused=(), count=0, sems=0, vmem=40, flops=1 << 26, size=1 << 22):
    def place(i, far):
        return pl.BlockSpec(memory_space=pltpu.SMEM if i in smem else pltpu.HBM if i in far else pltpu.VMEM)

    return pl.pallas_call(
        kernel,
        out_shape=[jax.ShapeDtypeStruct(shape, dtype) for shape, dtype in outs],
        in_specs=[place(i, hbm_in) for i in range(count)],
        out_specs=[
            pl.BlockSpec(memory_space=pltpu.HBM if i in hbm_out else pltpu.VMEM) for i in range(len(outs))
        ],
        scratch_shapes=[pltpu.VMEM(shape, dtype) for shape, dtype in scratch]
        + ([pltpu.SemaphoreType.DMA((sems,))] if sems else []),
        compiler_params=pltpu.CompilerParams(
            vmem_limit_bytes=vmem * 2**20,
            allow_input_fusion=[i in fused for i in range(count)] if fused else None,
        ),
        cost_estimate=pl.CostEstimate(flops=flops, bytes_accessed=size, transcendentals=0),
    )


def shifted(array, by):
    devices = lax.axis_size(CTX)
    pairs = [(i, i + by) for i in range(devices) if 0 <= i + by < devices]
    return lax.ppermute(array, CTX, pairs)


def per_device(x_in, bc_in, conv_x, conv_bc, log_decay, grad_y):
    core = lax.axis_index("core")
    owners = lax.axis_size(("x", "zh"))
    places = lax.axis_size(CTX)
    groups = bc_in.shape[1] // (2 * STATE)
    own = bc_in.shape[0]
    fan = owners // groups
    group = lax.axis_index(("x", "zh")) // fan
    taps_bc = lax.dynamic_slice_in_dim(conv_bc, group * (2 * STATE), 2 * STATE, 1)
    swap = [(0, 1), (1, 0)]

    (spread,) = call(
        fan_kernel, [((owners, own, 2 * STATE), BF16)], hbm_in=(0,), count=1, sems=owners, vmem=62
    )(bc_in)
    mine = lax.all_to_all(spread, ("x", "zh"), 0, 0, tiled=True)
    x_prev = shifted(x_in[ROWS - HALO :], 1)
    wide = (ROWS, COLS)
    padded = ((ROWS + 8, COLS), F32)
    store = (STORE,) + wide
    ge_hi, ge_lo, cum, cumt = call(
        decay_kernel, [(wide, BF16)] * 2 + [((ROWS, LANES), F32), ((BLOCKS, HEADS, BLOCK), F32)], count=2
    )(log_decay.T, grad_y)
    made = call(
        feature_kernel, [(store, F32)] + [(wide, BF16)] * 2, [padded, (wide, F32), (wide, F32)],
        hbm_out=(0,), count=4, sems=2,
    )(x_in, x_prev, conv_x, cum)
    mine, made = lax.optimization_barrier((mine, made))
    features, xf_hi, xf_lo = made
    scaled = (xf_hi, xf_lo, ge_hi, ge_lo)
    bc_prev = [
        lax.ppermute(
            mine[owners - 1], CTX + ("core",), [(2 * i + 1, 2 * (i + 1) + to) for i in range(places - 1)]
        )
        for to in (0, 1)
    ]
    bc_rows = lax.all_gather(mine, "core")
    packed = (places, piece_rows(STATE // places), LANES)
    (sent,) = call(functools.partial(state_kernel, places), [(packed, F32)], [padded], count=9)(
        bc_rows, *bc_prev, taps_bc, *scaled, cum
    )
    got = lax.all_to_all(sent.astype(jnp.float16), CTX, 0, 0, tiled=True)
    (early,) = call(
        first_kernel, [(store, F32)],
        [(wide, F32)] * 5 + [((ROWS, LANES), F32)] + [(wide, BF16)] * 2 + [padded],
        hbm_in=(0,), hbm_out=(0,), count=8, sems=6, flops=1 << 32,
    )(features, grad_y, bc_rows, *bc_prev, taps_bc, cum, cumt)
    got, early = lax.optimization_barrier((got, early))
    (back,) = call(functools.partial(scan_kernel, places), [(packed, F32)], fused=(0,), count=1)(got.astype(F32))
    early, back = lax.optimization_barrier((early, back))
    (blocks,) = call(
        second_kernel, [(store, F32)],
        [(wide, F32)] * 5 + [((ROWS, LANES), F32)] + [(wide, BF16)] * 2,
        hbm_in=(0, 1), hbm_out=(0,), count=5, sems=11, flops=1 << 32,
    )(features, early, grad_y, cum, cumt)
    carried = lax.all_to_all(back.astype(jnp.float16), CTX, 0, 0, tiled=True).astype(F32)

    half = (STATE, COLS)
    top = (HALO, COLS)
    pair = ((2,) + wide, BF16)
    states, both, first = call(
        functools.partial(open_kernel, places),
        [((2 * STORE,) + wide, BF16), ((8, COLS), F32), ((8, COLS + 2 * STATE), F32)],
        [(half, F32)] * 2 + [pair] + [(top, F32)] * 5,
        hbm_in=(6, 7), hbm_out=(0,), fused=(0,), count=8, sems=6,
    )(carried, *scaled, cum, features, blocks)
    halo = shifted(first, -1)
    (gbc,) = call(
        group_kernel, [(wide, F32)], [pair] + [(wide, F32)] * 2, hbm_in=(4, 5), count=6, sems=3
    )(*scaled, blocks, states)
    piece = (owners, own, 2 * STATE)
    keep, give = call(
        functools.partial(grad_bc_kernel, own), [(piece, F32)] * 2, [padded, (wide, F32)], smem=(0,), count=4
    )(core.reshape(1), gbc, halo, taps_bc)
    (summed,) = call(sum_kernel, [((owners, term_rows(own), LANES), F32)], count=2)(
        keep, lax.ppermute(give, "core", swap)
    )
    parts = lax.all_to_all(summed.astype(jnp.float16), ("x", "zh"), 0, 0, tiled=True).astype(F32)
    grad_x, glog = call(
        carry_kernel,
        [(wide, BF16), ((HEADS, ROWS), F32)],
        [padded, pair] + [(wide, F32)] * 3 + [((ROWS, LANES), F32)],
        hbm_in=(5, 6, 7), count=11, sems=5,
    )(*scaled, cum, features, blocks, states, both, halo, conv_x)
    (grad_bc,) = call(fold_kernel, [((own, groups * 2 * STATE), F32)], fused=(0,), count=1)(parts)
    return grad_x, grad_bc, glog.T


def solution(mesh):
    fine = Mesh(mesh.devices.reshape(8, 2, 4, 4, 2), CTX + TP)
    return jax.shard_map(
        per_device,
        mesh=fine,
        in_specs=(P(CTX, TP), P(CTX + TP, None), P(None, TP), P(), P(CTX, TP), P(CTX, TP)),
        out_specs=(P(CTX, TP), P(CTX + TP, None), P(CTX, TP)),
        check_vma=False,
    )
```
